32 devices in a mesh: grp: 2 (over y), comp: 16 (over z, x, core).
Axes of the slice: x: 2, y: 2, z: 4, core: 2. Of those that a mesh axis runs over, the one named last changes fastest.
Arguments:
- features: bfloat16 [65536, 256], P(('grp', 'comp')), may hold values from -8 to 8
- means: float32 [1024, 256], P('comp'), may hold values from -1 to 1
- variances: float32 [1024, 256], P('comp'), may hold values from 0.5 to 2
- weight_logits: float32 [1024], replicated, may hold values from -1 to 1
Outputs:
- new_means: float32 [1024, 256], replicated
- new_variances: float32 [1024, 256], replicated
- new_log_weights: float32 [1024], replicated
- row_scores: float32 [65536], P(('grp', 'comp'))
The draws below stay inside these ranges and needn't reach their ends.
All inputs are finite; a program needn't handle non-finite values.
Results may differ from the reference program's by a relative error of at most 0.00085.
Values sent between devices are 32-bit elements; how exact they have to be, the bound alone decides.
No kernel may reach another device: no remote copies, remote signals or barrier semaphores. Data moves between devices by JAX's collectives and lax.ppermute only.
A program may use at most 64 MiB of HBM per device.

```python
import math
import jax
import jax.numpy as jnp
from jax import lax

K = 1024
D = 256
ROWS_DEV = 2048
ROWS = 65536


def center_table(key):
    center_key = jax.random.fold_in(key, 11)
    return 0.15 * jnp.clip(jax.random.normal(center_key, (K, D), jnp.float32), -4.0, 4.0)


def draw_features(key, part):
    centers = center_table(key)
    offset_draw = jax.random.randint(jax.random.fold_in(key, 12), (ROWS,), 0, 16)
    block_index = jnp.arange(ROWS, dtype=jnp.int32) // ROWS_DEV
    cluster = (block_index * 2 + offset_draw) % K
    base_rows = centers[cluster]
    noise_key = jax.random.fold_in(key, 13)
    noise = jnp.clip(jax.random.normal(noise_key, (ROWS, D), jnp.float32), -5.0, 5.0)
    values = base_rows + noise
    return values.astype(jnp.bfloat16)


def draw_means(key, part):
    centers = center_table(key)
    shift_key = jax.random.fold_in(key, 15)
    shift = 0.05 * jnp.clip(jax.random.normal(shift_key, (K, D), jnp.float32), -4.0, 4.0)
    return centers + shift


def shard_levels(rng, extent, cuts, least, top_value):
    loudness = 1.0
    for axis_at, parts in cuts:
        heights = jax.random.uniform(jax.random.fold_in(jax.random.fold_in(rng, 6), axis_at), (parts,), jnp.float32, least / len(cuts), top_value / len(cuts))
        loudness = loudness * jnp.repeat(jnp.exp(heights), extent[axis_at] // parts).reshape((-1,) + (1,) * (len(extent) - 1 - axis_at))
    return loudness


def setup_inputs(seed: int = 0) -> dict:
    splits = jax.random.split(jax.random.key(seed), 5)
    return {
        "features": draw_features(jax.random.fold_in(splits[4], 71), 0),
        "means": draw_means(jax.random.fold_in(splits[4], 71), 0),
        "variances": jnp.clip(jnp.exp(math.log(2.0) - 1.3862944 * jax.random.uniform(splits[2], (K, D), jnp.float32) ** shard_levels(splits[2], (K, D), ((0, 16),), -0.2, 0.2)), 0.5, 2.0),
        "weight_logits": jnp.clip(jax.random.uniform(splits[3], (K,), jnp.float32, -1.0, 1.0), -1.0, 1.0),
    }


def update_step(moments, counts, total_rows):
    width = moments.shape[1] // 2
    denominator = (counts + 1.0)[:, None]
    fresh_means = moments[:, :width] / denominator
    fresh_variances = (moments[:, width:] + 1.0) / denominator - fresh_means * fresh_means + 0.01
    fresh_weights = jnp.log((counts + 1.0) / total_rows)
    return fresh_means, fresh_variances, fresh_weights


def reference(features, means, variances, weight_logits):
    inverse = 1.0 / variances
    coefficient = jnp.concatenate([-0.5 * inverse, means * inverse], axis=1)
    offsets = jax.nn.log_softmax(weight_logits) - 0.5 * jnp.sum(jnp.log(variances) + means * means * inverse, axis=1) - 0.5 * D * math.log(2.0 * math.pi)
    blocks = features.reshape(ROWS // ROWS_DEV, ROWS_DEV, D)

    def visit(accumulated, block_rows):
        moments, counts = accumulated
        values = block_rows.astype(jnp.float32)
        squared = values * values
        scores = jnp.dot(jnp.concatenate([squared, values], axis=1), coefficient.T, precision=lax.Precision.HIGHEST) + offsets
        highest = jnp.max(scores, axis=1, keepdims=True)
        exponent = jnp.exp(scores - highest)
        totals = jnp.sum(exponent, axis=1, keepdims=True)
        responsibility = (exponent / totals).astype(jnp.bfloat16)
        block_scores = (highest[:, 0] + jnp.log(totals[:, 0])) / D
        moment_inputs = jnp.concatenate([block_rows, squared.astype(jnp.bfloat16)], axis=1)
        moments = moments + jnp.dot(responsibility.T, moment_inputs, preferred_element_type=jnp.float32)
        counts = counts + jnp.dot(jnp.ones((ROWS_DEV,), jnp.bfloat16), responsibility, preferred_element_type=jnp.float32)
        return (moments, counts), block_scores

    start_state = (jnp.zeros((K, 2 * D), jnp.float32), jnp.zeros((K,), jnp.float32))
    (moments, counts), scores_all = lax.scan(visit, start_state, blocks)
    fresh_means, fresh_variances, fresh_weights = update_step(moments, counts, jnp.float32(ROWS + K))
    return fresh_means, fresh_variances, fresh_weights, scores_all.reshape(ROWS)
```

```python
import functools
import math

import jax
import jax.numpy as jnp
import numpy as np
from jax import lax
from jax.experimental import pallas as pl
from jax.experimental.pallas import tpu as pltpu
from jax.sharding import PartitionSpec as P

F32 = jnp.float32
BF16 = jnp.bfloat16
LANES = 128
COUNT_ROWS = 8
LOG2E = math.log2(math.e)
LN2 = math.log(2.0)


class Plan:
    def __init__(self, groups, owners, comps):
        self.devices = groups * owners
        self.owners = owners
        owner_bits = owners.bit_length() - 1
        group_bits = groups.bit_length() - 1
        assert owners == 1 << owner_bits and groups == 1 << group_bits and owner_bits >= 3
        self.piece = comps // owners
        self.unit = max(comps // self.devices, min(16, self.piece))
        splits = (comps // self.unit).bit_length() - 1
        group_split = splits - owner_bits
        grp = [owner_bits + b for b in range(group_bits)]
        rest = [1] + grp[:group_split] + list(range(2, owner_bits))
        swapped = [rest[1], rest[0]] + rest[2:]
        self.halving = [(0, 0)] + list(zip(rest, swapped))
        self.whole = [(b, b) for b in grp[group_split:]]
        down = list(range(owner_bits - 1, 0, -1))
        self.gather = list(zip(down, down[:-2] + [down[-1], down[-2]]))
        self.units = comps // self.unit
        per = self.piece // self.unit
        n = self.devices
        gather_at = np.zeros((n, owners), np.int32)
        slot_chunk = np.zeros((n, self.units), np.int32)
        steps = self.gather + [(0, 0)]
        for d in range(n):
            for p in range(owners):
                e = d
                for t in reversed(range(len(steps))):
                    if p >> t & 1:
                        e ^= 1 << steps[t][e & 1]
                gather_at[d, p] = e % owners
            for j in range(self.units):
                e = d
                for s, step in enumerate(self.halving):
                    if j >> (splits - 1 - s) & 1:
                        e ^= 1 << step[e & 1]
                slot_chunk[d, j] = (e % owners) * per + (e // owners) % per
        unit_chunk = (gather_at[:, :, None] * per + np.arange(per)).reshape(n, self.units)
        chunk_slot = np.argsort(slot_chunk, axis=1)
        unit_slot = np.take_along_axis(chunk_slot, unit_chunk, axis=1)
        self.tables = np.stack([unit_chunk, unit_slot, slot_chunk], axis=1).astype(np.int32)

    def pairs(self, step):
        return [(d, d ^ (1 << step[d & 1])) for d in range(self.devices)]

    def swap(self, value, step):
        return lax.ppermute(value, ("grp", "comp"), self.pairs(step))


def columns(row, height):
    return jnp.broadcast_to(row, (height, LANES)).T


def features_kernel(rows_ref, stack_ref, inputs_ref):
    rows = rows_ref[...]
    values = rows.astype(F32)
    squares = values * values
    high = squares.astype(BF16)
    low = (squares - high.astype(F32)).astype(BF16)
    width = rows.shape[1]
    high_t, low_t, rows_t = high.T, low.T, rows.T
    for at, part in enumerate((low_t, high_t, rows_t, high_t, rows_t)):
        stack_ref[at * width : (at + 1) * width, :] = part
    inputs_ref[:, :width] = rows
    inputs_ref[:, width:] = high


def prepare_features(features):
    count, width = features.shape
    block = min(512, count)
    return pl.pallas_call(
        features_kernel,
        grid=(count // block,),
        in_specs=[pl.BlockSpec((block, width), lambda i: (i, 0))],
        out_specs=[
            pl.BlockSpec((5 * width, block), lambda i: (0, i)),
            pl.BlockSpec((block, 2 * width), lambda i: (i, 0)),
        ],
        out_shape=[
            jax.ShapeDtypeStruct((5 * width, count), BF16),
            jax.ShapeDtypeStruct((count, 2 * width), BF16),
        ],
        compiler_params=pltpu.CompilerParams(vmem_limit_bytes=48 * 2**20),
        cost_estimate=pl.CostEstimate(flops=8 * count * width, bytes_accessed=16 * count * width, transcendentals=0),
    )(features)


def mixture_kernel(plan, pieces, table, *refs):
    logits_ref, stack_ref, inputs_ref = refs[pieces : pieces + 3]
    sent_ref, kept_ref, scores_ref = refs[pieces + 3 : pieces + 6]
    weights, offsets, moments, partial, staged = refs[pieces + 6 :]
    comps, depth = weights.shape
    width = depth // 5
    unit = plan.unit
    step = pl.program_id(0)

    @pl.when(step == 0)
    def _():
        logits = logits_ref[...]
        top = jnp.max(logits)
        shifted = logits - top
        log_weights = shifted - jnp.log(jnp.sum(jnp.exp(shifted)))
        for b in range(comps // LANES):
            staged[b * LANES : (b + 1) * LANES, :] = columns(log_weights[b : b + 1, :], LANES)
        at = 0
        for ref in refs[:pieces]:
            for first in range(0, ref.shape[0], unit):
                here = slice(at, at + unit)
                mean = ref[first : first + unit, :width]
                variance = ref[first : first + unit, width:]
                inverse = 1.0 / variance
                linear = mean * inverse
                constant = jnp.sum(jnp.log(variance) + mean * linear, axis=1, keepdims=True)
                chunk = pl.multiple_of(table[0, at // unit] * unit, unit)
                log_weight = staged[pl.ds(chunk, unit), :]
                offsets[here, :] = (
                    log_weight - 0.5 * constant - 0.5 * width * math.log(2.0 * math.pi)
                ) * LOG2E
                square = inverse * (-0.5 * LOG2E)
                linear = linear * LOG2E
                square_high = square.astype(BF16)
                linear_high = linear.astype(BF16)
                weights[here, :width] = square_high
                weights[here, width : 2 * width] = square_high
                weights[here, 2 * width : 3 * width] = linear_high
                weights[here, 3 * width : 4 * width] = (square - square_high.astype(F32)).astype(BF16)
                weights[here, 4 * width :] = (linear - linear_high.astype(F32)).astype(BF16)
                at += unit
        moments[...] = jnp.zeros_like(moments)
        partial[...] = jnp.zeros_like(partial)

    block = stack_ref.shape[1]
    scores = jnp.dot(weights[...], stack_ref[...], preferred_element_type=F32)
    scores = scores + jnp.tile(offsets[...], (1, block // LANES))
    highest = jnp.max(scores, axis=0, keepdims=True)
    exponent = jnp.exp2(scores - highest)
    totals = jnp.sum(exponent, axis=0, keepdims=True)
    responsibility = (exponent * (1.0 / totals)).astype(BF16)
    scores_ref[...] = ((highest + jnp.log2(totals)) * (LN2 / width)).reshape(scores_ref.shape)
    moments[...] += jnp.dot(responsibility, inputs_ref[...], preferred_element_type=F32)
    rounded = responsibility.astype(F32)
    counted = rounded[:, :LANES]
    for b in range(1, block // LANES):
        counted = counted + rounded[:, b * LANES : (b + 1) * LANES]
    partial[...] += counted

    @pl.when(step == pl.num_programs(0) - 1)
    def _():
        parts = 2 * width // LANES
        half = comps // 2 * parts
        for u in range(comps // unit):
            chunk = pl.multiple_of(table[0, u] * unit, unit)
            staged[pl.ds(chunk, unit), :] = partial[u * unit : (u + 1) * unit, :]
        for b in range(comps // LANES):
            line = jnp.sum(staged[b * LANES : (b + 1) * LANES, :].T, axis=0, keepdims=True)
            sent_ref[half + b : half + b + 1, :] = line
            kept_ref[half + b : half + b + 1, :] = line
        for u in range(comps // unit):
            target = kept_ref if u < comps // unit // 2 else sent_ref
            slot = table[1, u] % (comps // unit // 2)
            first = pl.multiple_of(slot * unit * parts, unit)
            for part in range(parts):
                target[pl.ds(first + part * unit, unit), :] = moments[
                    u * unit : (u + 1) * unit, part * LANES : (part + 1) * LANES
                ]


def mixture(plan, table, parameters, logits, stack, inputs):
    depth, count = stack.shape
    width = depth // 5
    comps = sum(p.shape[0] for p in parameters)
    block = min(512, count)
    half = comps // 2 * (2 * width // LANES) + COUNT_ROWS
    whole = lambda shape: pl.BlockSpec(shape, lambda i, t: (0,) * len(shape))
    return pl.pallas_call(
        functools.partial(mixture_kernel, plan, len(parameters)),
        grid_spec=pltpu.PrefetchScalarGridSpec(
            num_scalar_prefetch=1,
            grid=(count // block,),
            in_specs=[whole(p.shape) for p in parameters]
            + [
                whole(logits.shape),
                pl.BlockSpec((depth, block), lambda i, t: (0, i)),
                pl.BlockSpec((block, 2 * width), lambda i, t: (i, 0)),
            ],
            out_specs=[
                whole((half, LANES)),
                whole((half, LANES)),
                pl.BlockSpec((1, block), lambda i, t: (0, i)),
            ],
            scratch_shapes=[
                pltpu.VMEM((comps, depth), BF16),
                pltpu.VMEM((comps, LANES), F32),
                pltpu.VMEM((comps, 2 * width), F32),
                pltpu.VMEM((comps, LANES), F32),
                pltpu.VMEM((comps, LANES), F32),
            ],
        ),
        out_shape=[
            jax.ShapeDtypeStruct((half, LANES), F32),
            jax.ShapeDtypeStruct((half, LANES), F32),
            jax.ShapeDtypeStruct((1, count), F32),
        ],
        compiler_params=pltpu.CompilerParams(vmem_limit_bytes=56 * 2**20),
        cost_estimate=pl.CostEstimate(
            flops=14 * comps * count * width, bytes_accessed=12 * 2**20, transcendentals=comps * count
        ),
    )(table, *parameters, logits, stack, inputs)


def update_kernel(plan, pieces, total_rows, table, *refs):
    counts_ref = refs[pieces]
    means_ref, variances_ref, log_weights_ref = refs[pieces + 1 : pieces + 4]
    staged = refs[pieces + 4]
    comps, width = means_ref.shape
    unit = plan.unit
    parts = width // LANES
    denominator = counts_ref[...] + 1.0
    log_weights_ref[...] = jnp.log(denominator / total_rows)
    inverse = 1.0 / denominator
    for b in range(comps // LANES):
        staged[b * LANES : (b + 1) * LANES, :] = columns(inverse[b : b + 1, :], LANES)
    slot = 0
    for ref in refs[:pieces]:
        for first in range(0, ref.shape[0], unit * 2 * parts):
            chunk = pl.ds(pl.multiple_of(table[2, slot] * unit, unit), unit)
            scale = staged[chunk, :]
            for part in range(parts):
                lanes = slice(part * LANES, (part + 1) * LANES)
                at = first + part * unit
                mean = ref[at : at + unit, :] * scale
                at += parts * unit
                means_ref[chunk, lanes] = mean
                variances_ref[chunk, lanes] = (ref[at : at + unit, :] + 1.0) * scale - mean * mean + 0.01
            slot += 1


def update(plan, table, moments, counts, comps, width, total_rows):
    whole = lambda shape: pl.BlockSpec(shape, lambda i, t: (0,) * len(shape))
    shapes = [(comps, width), (comps, width), counts.shape]
    return pl.pallas_call(
        functools.partial(update_kernel, plan, len(moments), total_rows),
        grid_spec=pltpu.PrefetchScalarGridSpec(
            num_scalar_prefetch=1,
            grid=(1,),
            in_specs=[whole(m.shape) for m in moments] + [whole(counts.shape)],
            out_specs=[whole(s) for s in shapes],
            scratch_shapes=[pltpu.VMEM((comps, LANES), F32)],
        ),
        out_shape=[jax.ShapeDtypeStruct(s, F32) for s in shapes],
        compiler_params=pltpu.CompilerParams(vmem_limit_bytes=32 * 2**20),
        cost_estimate=pl.CostEstimate(flops=8 * comps * width, bytes_accessed=16 * comps * width, transcendentals=0),
    )(table, *moments, counts)


def on_device(plan, features, means, variances, weight_logits):
    comps = weight_logits.shape[0]
    width = means.shape[1]
    me = lax.axis_index(("grp", "comp"))
    table = lax.dynamic_index_in_dim(jnp.asarray(plan.tables), me, 0, keepdims=False)
    stack, inputs = prepare_features(features)

    with jax.named_scope("gather_parameters"):
        parameters = [jnp.concatenate([means, variances], axis=1)]
        for step in plan.gather:
            held = parameters[0] if len(parameters) == 1 else jnp.concatenate(parameters, axis=0)
            parameters.append(plan.swap(held, step))
        parameters += [plan.swap(p, (0, 0)) for p in parameters]

    sent, kept, row_scores = mixture(
        plan, table, parameters, weight_logits.reshape(comps // LANES, LANES), stack, inputs
    )

    with jax.named_scope("scatter_moments"):
        counts = kept[-COUNT_ROWS:]
        kept = kept[:-COUNT_ROWS]
        for at, step in enumerate(plan.halving):
            arrived = plan.swap(sent, step)
            kept = kept + arrived[:-COUNT_ROWS]
            counts = counts + arrived[-COUNT_ROWS:]
            if at + 1 < len(plan.halving):
                half = kept.shape[0] // 2
                sent = jnp.concatenate([kept[half:], counts], axis=0)
                kept = kept[:half]
        for step in plan.whole:
            arrived = plan.swap(jnp.concatenate([kept, counts], axis=0), step)
            kept = kept + arrived[:-COUNT_ROWS]
            counts = counts + arrived[-COUNT_ROWS:]

    with jax.named_scope("gather_moments"):
        moments = [kept]
        for step in reversed(plan.halving[1:]):
            held = moments[0] if len(moments) == 1 else jnp.concatenate(moments, axis=0)
            moments.append(plan.swap(held, step))
        moments += [plan.swap(m, (0, 0)) for m in moments]

    total_rows = float(features.shape[0] * plan.devices + comps)
    fresh_means, fresh_variances, fresh_weights = update(
        plan, table, moments, counts, comps, width, total_rows
    )
    return fresh_means, fresh_variances, fresh_weights.reshape(comps), row_scores.reshape(-1)


def solution(mesh):
    def whole(features, means, variances, weight_logits):
        plan = Plan(mesh.shape["grp"], mesh.shape["comp"], weight_logits.shape[0])
        return jax.shard_map(
            functools.partial(on_device, plan),
            mesh=mesh,
            in_specs=(P(("grp", "comp"), None), P("comp", None), P("comp", None), P()),
            out_specs=(P(), P(), P(), P(("grp", "comp"))),
            check_vma=False,
        )(features, means, variances, weight_logits)

    return whole
```

```python
import functools
import math

import jax
import jax.numpy as jnp
import numpy as np
from jax import lax
from jax.experimental import pallas as pl
from jax.experimental.pallas import tpu as pltpu
from jax.sharding import PartitionSpec as P

F32 = jnp.float32
BF16 = jnp.bfloat16
LANES = 128
COUNT_ROWS = 8
LOG2E = math.log2(math.e)
LN2 = math.log(2.0)
BLOCK = 1024
VMEM_MIB = 40


class Plan:
    def __init__(self, groups, owners, comps):
        self.devices = groups * owners
        self.owners = owners
        owner_bits = owners.bit_length() - 1
        group_bits = groups.bit_length() - 1
        assert owners == 1 << owner_bits and groups == 1 << group_bits and owner_bits >= 4
        piece = comps // owners
        self.unit = max(comps // self.devices, min(16, piece))
        self.units = comps // self.unit
        per = piece // self.unit
        splits = self.units.bit_length() - 1
        group_split = splits - owner_bits
        grp = [owner_bits + b for b in range(group_bits)]
        first, second, third, *others = [1] + grp[:group_split] + list(range(2, owner_bits))
        orders = (
            ((first, second, third), (third, first, second)),
            ((second, third, first), (second, first, third)),
        )
        self.halving = [
            [(0, 0)] + list(zip(zero, one)) + [(b, b) for b in others] for zero, one in orders
        ]
        self.whole = [(b, b) for b in grp[group_split:]]
        down = list(range(owner_bits - 1, 0, -1))
        self.gather = list(zip(down, down[:-2] + [down[-1], down[-2]]))
        n = self.devices
        gather_at = np.zeros((n, owners), np.int32)
        slot_chunk = np.zeros((2, n, self.units), np.int32)
        steps = self.gather + [(0, 0)]
        for d in range(n):
            for p in range(owners):
                e = d
                for t in reversed(range(len(steps))):
                    if p >> t & 1:
                        e ^= 1 << steps[t][e & 1]
                gather_at[d, p] = e % owners
            for stream, halving in enumerate(self.halving):
                for j in range(self.units):
                    e = d
                    for s, step in enumerate(halving):
                        if j >> (splits - 1 - s) & 1:
                            e ^= 1 << step[e & 1]
                    slot_chunk[stream, d, j] = (e % owners) * per + (e // owners) % per
        unit_chunk = (gather_at[:, :, None] * per + np.arange(per)).reshape(n, self.units)
        unit_slot = [np.take_along_axis(np.argsort(c, axis=1), unit_chunk, axis=1) for c in slot_chunk]
        self.tables = np.stack([unit_chunk, *unit_slot, *slot_chunk], axis=1).astype(np.int32)

    def swap(self, value, step):
        pairs = [(d, d ^ (1 << step[d & 1])) for d in range(self.devices)]
        return lax.ppermute(value, ("grp", "comp"), pairs)


def columns(row, height):
    return jnp.broadcast_to(row, (height, LANES)).T


def mixture_kernel(plan, pieces, block, table, *refs):
    mean_refs, variance_refs = refs[:pieces], refs[pieces : 2 * pieces]
    logits_ref, features_ref = refs[2 * pieces : 2 * pieces + 2]
    sent_refs = refs[2 * pieces + 2 : 2 * pieces + 4]
    kept_refs = refs[2 * pieces + 4 : 2 * pieces + 6]
    scores_ref = refs[2 * pieces + 6]
    weights, offsets, moments, partial, staged = refs[2 * pieces + 7 :]
    comps = weights.shape[0]
    count, width = features_ref.shape
    unit = plan.unit

    logits = logits_ref[...]
    shifted = logits - jnp.max(logits)
    log_weights = shifted - jnp.log(jnp.sum(jnp.exp(shifted)))
    for b in range(comps // LANES):
        staged[b * LANES : (b + 1) * LANES, :] = columns(log_weights[b : b + 1, :], LANES)
    at = 0
    for mean_ref, variance_ref in zip(mean_refs, variance_refs):
        for first in range(0, mean_ref.shape[0], unit):
            here = slice(at, at + unit)
            mean = mean_ref[first : first + unit, :]
            variance = variance_ref[first : first + unit, :]
            inverse = 1.0 / variance
            linear = mean * inverse
            constant = jnp.sum(jnp.log(variance) + mean * linear, axis=1, keepdims=True)
            chunk = pl.multiple_of(table[0, at // unit] * unit, unit)
            log_weight = staged[pl.ds(chunk, unit), :]
            offsets[here, :] = (
                log_weight - 0.5 * constant - 0.5 * width * math.log(2.0 * math.pi)
            ) * LOG2E
            square = inverse * (-0.5 * LOG2E)
            linear = linear * LOG2E
            square_high = square.astype(BF16)
            linear_high = linear.astype(BF16)
            weights[here, :width] = square_high
            weights[here, width : 2 * width] = square_high
            weights[here, 2 * width : 3 * width] = linear_high
            weights[here, 3 * width : 4 * width] = (square - square_high.astype(F32)).astype(BF16)
            weights[here, 4 * width :] = (linear - linear_high.astype(F32)).astype(BF16)
            at += unit

    for first in range(0, count, block):
        rows = features_ref[first : first + block, :]
        values = rows.astype(F32)
        squares = values * values
        high = squares.astype(BF16)
        low = (squares - high.astype(F32)).astype(BF16)
        scores = lax.dot_general(
            weights[...],
            jnp.concatenate([low, high, rows, high, rows], axis=1),
            (((1,), (1,)), ((), ())),
            preferred_element_type=F32,
        )
        scores = scores + jnp.tile(offsets[...], (1, block // LANES))
        highest = jnp.max(scores, axis=0, keepdims=True)
        exponent = jnp.exp2(scores - highest)
        totals = jnp.sum(exponent, axis=0, keepdims=True)
        responsibility = (exponent * (1.0 / totals)).astype(BF16)
        scores_ref[:, first : first + block] = (highest + jnp.log2(totals)) * (LN2 / width)
        added = jnp.dot(
            responsibility, jnp.concatenate([rows, high], axis=1), preferred_element_type=F32
        )
        rounded = responsibility.astype(F32)
        counted = rounded[:, :LANES]
        for b in range(1, block // LANES):
            counted = counted + rounded[:, b * LANES : (b + 1) * LANES]
        if first == 0:
            moments[...] = added
            partial[...] = counted
        else:
            moments[...] += added
            partial[...] += counted

    parts = width // LANES
    units = comps // unit
    half = comps // 2 * parts
    for u in range(units):
        chunk = pl.multiple_of(table[0, u] * unit, unit)
        staged[pl.ds(chunk, unit), :] = partial[u * unit : (u + 1) * unit, :]
    for b in range(comps // LANES):
        line = jnp.sum(staged[b * LANES : (b + 1) * LANES, :].T, axis=0, keepdims=True)
        sent_refs[0][half + b : half + b + 1, :] = line
        kept_refs[0][half + b : half + b + 1, :] = line
    for u in range(units):
        targets = kept_refs if u < units // 2 else sent_refs
        for stream, target in enumerate(targets):
            first = pl.multiple_of(table[1 + stream, u] % (units // 2) * (unit * parts), unit)
            for part in range(parts):
                at = stream * width + part * LANES
                target[pl.ds(first + part * unit, unit), :] = moments[
                    u * unit : (u + 1) * unit, at : at + LANES
                ]


def mixture(plan, table, means, variances, logits, features):
    count, width = features.shape
    comps = sum(p.shape[0] for p in means)
    half = comps // 2 * (width // LANES)
    shapes = [(half + COUNT_ROWS, LANES), (half, LANES)] * 2 + [(1, count)]
    vmem = pl.BlockSpec(memory_space=pltpu.VMEM)
    outs = pl.pallas_call(
        functools.partial(mixture_kernel, plan, len(means), min(BLOCK, count)),
        in_specs=[pl.BlockSpec(memory_space=pltpu.SMEM)] + [vmem] * (2 * len(means) + 2),
        out_specs=[vmem] * 5,
        out_shape=[jax.ShapeDtypeStruct(s, F32) for s in shapes],
        scratch_shapes=[
            pltpu.VMEM((comps, 5 * width), BF16),
            pltpu.VMEM((comps, LANES), F32),
            pltpu.VMEM((comps, 2 * width), F32),
            pltpu.VMEM((comps, LANES), F32),
            pltpu.VMEM((comps, LANES), F32),
        ],
        compiler_params=pltpu.CompilerParams(vmem_limit_bytes=VMEM_MIB * 2**20),
        cost_estimate=pl.CostEstimate(
            flops=14 * comps * count * width, bytes_accessed=8 * 2**20, transcendentals=comps * count
        ),
    )(table, *means, *variances, logits, features)
    return outs[:2], outs[2:4], outs[4]


def update_kernel(plan, pieces, total_rows, table, *refs):
    first_refs, second_refs = refs[:pieces], refs[pieces : 2 * pieces]
    counts_ref = refs[2 * pieces]
    means_ref, variances_ref, log_weights_ref, staged = refs[2 * pieces + 1 :]
    comps, width = means_ref.shape
    unit = plan.unit
    parts = width // LANES
    denominator = counts_ref[...] + 1.0
    log_weights_ref[...] = jnp.log(denominator / total_rows)
    inverse = 1.0 / denominator
    for b in range(comps // LANES):
        staged[b * LANES : (b + 1) * LANES, :] = columns(inverse[b : b + 1, :], LANES)
    for stream, stream_refs in enumerate((first_refs, second_refs)):
        slot = 0
        for ref in stream_refs:
            for first in range(0, ref.shape[0], unit * parts):
                chunk = pl.ds(pl.multiple_of(table[3 + stream, slot] * unit, unit), unit)
                scale = staged[chunk, :]
                for part in range(parts):
                    lanes = slice(part * LANES, (part + 1) * LANES)
                    moment = ref[first + part * unit : first + (part + 1) * unit, :]
                    if stream == 0:
                        means_ref[chunk, lanes] = moment * scale
                    else:
                        mean = means_ref[chunk, lanes]
                        variances_ref[chunk, lanes] = (moment + 1.0) * scale - mean * mean + 0.01
                slot += 1


def update(plan, table, first, second, counts, comps, width, total_rows):
    vmem = pl.BlockSpec(memory_space=pltpu.VMEM)
    shapes = [(comps, width), (comps, width), counts.shape]
    return pl.pallas_call(
        functools.partial(update_kernel, plan, len(first), total_rows),
        in_specs=[pl.BlockSpec(memory_space=pltpu.SMEM)] + [vmem] * (2 * len(first) + 1),
        out_specs=[vmem] * 3,
        scratch_shapes=[pltpu.VMEM((comps, LANES), F32)],
        out_shape=[jax.ShapeDtypeStruct(s, F32) for s in shapes],
        compiler_params=pltpu.CompilerParams(vmem_limit_bytes=16 * 2**20),
        cost_estimate=pl.CostEstimate(flops=8 * comps * width, bytes_accessed=16 * comps * width, transcendentals=0),
    )(table, *first, *second, counts)


def gather(plan, streams, steps):
    held = streams
    for step in steps[:-1]:
        held = [jnp.concatenate([h, plan.swap(h, at)], axis=0) for h, at in zip(held, step)]
    last = [plan.swap(h, at) for h, at in zip(held, steps[-1])]
    mates = [plan.swap(h, (0, 0)) for h in held]
    return [[h, l, m, plan.swap(l, (0, 0))] for h, l, m in zip(held, last, mates)]


def scatter(plan, sent, kept):
    rows = kept[1].shape[0]
    counts = kept[0][rows:]
    kept = [kept[0][:rows], kept[1]]
    for at, step in enumerate(zip(*plan.halving)):
        arrived = [plan.swap(s, pair) for s, pair in zip(sent, step)]
        counts = counts + arrived[0][rows:]
        kept = [k + a[:rows] for k, a in zip(kept, arrived)]
        if at + 1 < len(plan.halving[0]):
            rows //= 2
            sent = [jnp.concatenate([kept[0][rows:], counts], axis=0), kept[1][rows:]]
            kept = [k[:rows] for k in kept]
    for pair in plan.whole:
        arrived = [plan.swap(jnp.concatenate([kept[0], counts], axis=0), pair), plan.swap(kept[1], pair)]
        counts = counts + arrived[0][rows:]
        kept = [k + a[:rows] for k, a in zip(kept, arrived)]
    return kept, 0.5 * (counts + plan.swap(counts, (0, 0)))


def on_device(plan, features, means, variances, weight_logits):
    comps = weight_logits.shape[0]
    width = means.shape[1]
    me = lax.axis_index(("grp", "comp"))
    table = lax.dynamic_index_in_dim(jnp.asarray(plan.tables), me, 0, keepdims=False)

    with jax.named_scope("gather_parameters"):
        all_means, all_variances = gather(plan, [means, variances], [(g, g) for g in plan.gather])
    sent, kept, row_scores = mixture(
        plan, table, all_means, all_variances, weight_logits.reshape(comps // LANES, LANES), features
    )
    with jax.named_scope("scatter_moments"):
        kept, counts = scatter(plan, sent, kept)
    with jax.named_scope("gather_moments"):
        first, second = gather(plan, kept, list(zip(*plan.halving))[:0:-1])

    total_rows = float(features.shape[0] * plan.devices + comps)
    fresh_means, fresh_variances, fresh_weights = update(
        plan, table, first, second, counts, comps, width, total_rows
    )
    return fresh_means, fresh_variances, fresh_weights.reshape(comps), row_scores.reshape(-1)


def solution(mesh):
    def whole(features, means, variances, weight_logits):
        plan = Plan(mesh.shape["grp"], mesh.shape["comp"], weight_logits.shape[0])
        return jax.shard_map(
            functools.partial(on_device, plan),
            mesh=mesh,
            in_specs=(P(("grp", "comp"), None), P("comp", None), P("comp", None), P()),
            out_specs=(P(), P(), P(), P(("grp", "comp"))),
            check_vma=False,
        )(features, means, variances, weight_logits)

    return whole
```

```python
import functools
import math

import jax
import jax.numpy as jnp
import numpy as np
from jax import lax
from jax.experimental import pallas as pl
from jax.experimental.pallas import tpu as pltpu
from jax.sharding import PartitionSpec as P

F32 = jnp.float32
BF16 = jnp.bfloat16
LANES = 128
COUNT_ROWS = 8
LOG2E = math.log2(math.e)
LN2 = math.log(2.0)
BLOCK = 1024


class Plan:
    def __init__(self, groups, owners, comps):
        self.devices = groups * owners
        self.owners = owners
        owner_bits = owners.bit_length() - 1
        group_bits = groups.bit_length() - 1
        assert owners == 1 << owner_bits and groups == 1 << group_bits and owner_bits >= 4
        piece = comps // owners
        group = list(range(owner_bits, owner_bits + group_bits))
        split = [1] + group[:1] + list(range(2, owner_bits - 1))
        while comps >> (len(split) + 1) < 16:
            split.pop()
        rest = [b for b in range(1, owner_bits + group_bits) if b not in split]
        self.units = 1 << (len(split) + 1)
        self.unit = comps // self.units
        assert piece % self.unit == 0
        per = piece // self.unit
        first, second, third, *others = split
        orders = (
            ((first, second, third), (third, first, second)),
            ((second, third, first), (second, first, third)),
        )
        self.halving = [
            [(0, 0)] + list(zip(zero, one)) + [(b, b) for b in others] for zero, one in orders
        ]
        self.whole = [(b, b) for b in rest]
        down = list(range(owner_bits - 1, 0, -1))
        self.gather = list(zip(down, down[:-2] + [down[-1], down[-2]]))

        def reach(device, steps, place):
            for t in reversed(range(len(steps))):
                if place >> t & 1:
                    device ^= 1 << steps[t][device & 1]
            return device

        n = range(self.devices)
        places = range(owners)
        gather_at = np.array([[reach(d, self.gather + [(0, 0)], p) % owners for p in places] for d in n])
        unit_chunk = (gather_at[:, :, None] * per + np.arange(per)).reshape(self.devices, self.units)
        owned = sorted([0] + split)
        slot_chunk = []
        for halving in self.halving:
            at = np.array([[reach(d, halving[::-1], j) for j in range(self.units)] for d in n])
            slot_chunk.append(sum((at >> b & 1) << i for i, b in enumerate(owned)))
        unit_slot = [np.take_along_axis(np.argsort(c, axis=1), unit_chunk, axis=1) for c in slot_chunk]
        self.tables = np.stack([unit_chunk, *unit_slot, *slot_chunk], axis=1).astype(np.int32)

    def swap(self, value, step):
        pairs = [(d, d ^ (1 << step[d & 1])) for d in range(self.devices)]
        return lax.ppermute(value, ("grp", "comp"), pairs)


def columns(row, height):
    return jnp.broadcast_to(row, (height, LANES)).T


def prepare_kernel(plan, table, *refs):
    sources, copies, (stack_ref, staged, features_ref, logits_ref, sems) = refs[:4], refs[4:6], refs[6:]
    targets = (features_ref, logits_ref, *copies)
    moves = [pltpu.make_async_copy(s, t, sems.at[i]) for i, (s, t) in enumerate(zip(sources, targets))]
    for move in moves:
        move.start()
    for move in moves:
        move.wait()
    logits = logits_ref[...]
    shifted = logits - jnp.max(logits)
    log_weights = shifted - jnp.log(jnp.sum(jnp.exp(shifted)))
    for b in range(logits.shape[0]):
        staged[b * LANES : (b + 1) * LANES, :] = columns(log_weights[b : b + 1, :], LANES)
    width = features_ref.shape[1]
    rows = features_ref[...]
    values = rows.astype(F32)
    squares = values * values
    high = squares.astype(BF16)
    stack_ref[:, :width] = (squares - high.astype(F32)).astype(BF16)
    stack_ref[:, width : 2 * width] = high
    stack_ref[:, 2 * width :] = rows


def build_weights(unit, table, first_units, mean_refs, variance_refs, log_weights, weights, offsets):
    at = 0
    width = mean_refs[0].shape[1]
    for mean_ref, variance_ref, first_unit in zip(mean_refs, variance_refs, first_units):
        for first in range(0, mean_ref.shape[0], unit):
            here = slice(at, at + unit)
            mean = mean_ref[first : first + unit, :]
            variance = variance_ref[first : first + unit, :]
            inverse = 1.0 / variance
            linear = mean * inverse
            constant = jnp.sum(jnp.log(variance) + mean * linear, axis=1, keepdims=True)
            chunk = pl.multiple_of(table[0, first_unit + first // unit] * unit, unit)
            log_weight = log_weights[pl.ds(chunk, unit), :]
            offsets[here, :] = (
                log_weight - 0.5 * constant - 0.5 * width * math.log(2.0 * math.pi)
            ) * LOG2E
            square = inverse * (-0.5 * LOG2E)
            linear = linear * LOG2E
            square_high = square.astype(BF16)
            linear_high = linear.astype(BF16)
            weights[here, :width] = square_high
            weights[here, width : 2 * width] = square_high
            weights[here, 2 * width : 3 * width] = linear_high
            weights[here, 3 * width : 4 * width] = (square - square_high.astype(F32)).astype(BF16)
            weights[here, 4 * width :] = (linear - linear_high.astype(F32)).astype(BF16)
            at += unit


def block_scores(stack, weights, offsets):
    width = stack.shape[1] // 3
    scores = lax.dot_general(
        weights[...],
        jnp.concatenate([stack, stack[:, width:]], axis=1),
        (((1,), (1,)), ((), ())),
        preferred_element_type=F32,
    )
    return scores + jnp.tile(offsets[...], (1, stack.shape[0] // LANES))


def store_moments(plan, table, first_unit, moments, targets):
    unit = plan.unit
    width = moments.shape[1] // 2
    parts = width // LANES
    for u in range(moments.shape[0] // unit):
        for column, target in enumerate(targets):
            slot = table[2 - column, first_unit + u] % (plan.units // 2)
            first = pl.multiple_of(slot * (unit * parts), unit)
            for part in range(parts):
                at = column * width + part * LANES
                target[pl.ds(first + part * unit, unit), :] = moments[
                    u * unit : (u + 1) * unit, at : at + LANES
                ]


def early_kernel(plan, table, *refs):
    mean_refs, variance_refs = refs[0:2], refs[2:4]
    log_weights, stack_ref, scores_ref = refs[4:7]
    weights, offsets = refs[7:]
    count = stack_ref.shape[0]
    block = min(BLOCK, count)
    firsts = (0, plan.units // 2)
    build_weights(plan.unit, table, firsts, mean_refs, variance_refs, log_weights, weights, offsets)
    for first in range(0, count, block):
        scores_ref[:, first : first + block] = block_scores(
            stack_ref[first : first + block, :], weights, offsets
        )


def late_kernel(plan, table, *refs):
    mean_refs, variance_refs = refs[0:2], refs[2:4]
    log_weights, stack_ref, early_ref = refs[4:7]
    sent_refs, counts_ref, scores_ref, own_ref = refs[7:9], refs[9], refs[10], refs[11]
    weights, offsets, moments, partial, staged = refs[12:]
    count, width = stack_ref.shape[0], stack_ref.shape[1] // 3
    block = min(BLOCK, count)
    quarter = weights.shape[0] // 2
    quarters = plan.units // 4
    firsts = (quarters, 3 * quarters)
    build_weights(plan.unit, table, firsts, mean_refs, variance_refs, log_weights, weights, offsets)
    for first in range(0, count, block):
        stack = stack_ref[first : first + block, :]
        late = block_scores(stack, weights, offsets)
        early = early_ref[:, first : first + block]
        highest = jnp.maximum(
            jnp.max(early, axis=0, keepdims=True), jnp.max(late, axis=0, keepdims=True)
        )
        early = jnp.exp2(early - highest)
        late = jnp.exp2(late - highest)
        totals = jnp.sum(early, axis=0, keepdims=True) + jnp.sum(late, axis=0, keepdims=True)
        scores_ref[:, first : first + block] = (highest + jnp.log2(totals)) * (LN2 / width)
        inverse = 1.0 / totals
        early = (early * inverse).astype(BF16)
        late = (late * inverse).astype(BF16)
        own_ref[:quarter, first : first + block] = early[:quarter]
        own_ref[quarter:, first : first + block] = late[:quarter]
        added = jnp.dot(
            jnp.concatenate([early[quarter:], late[quarter:]], axis=0),
            stack[:, width:],
            preferred_element_type=F32,
        )
        if first == 0:
            moments[...] = added
        else:
            moments[...] += added
        for at, part in enumerate((early[:quarter], late[:quarter], early[quarter:], late[quarter:])):
            rounded = part.astype(F32)
            counted = rounded[:, :LANES]
            for b in range(1, block // LANES):
                counted = counted + rounded[:, b * LANES : (b + 1) * LANES]
            here = slice(at * quarter, (at + 1) * quarter)
            if first == 0:
                partial[here, :] = counted
            else:
                partial[here, :] += counted

    unit = plan.unit
    for u in range(plan.units):
        chunk = pl.multiple_of(table[0, u] * unit, unit)
        staged[pl.ds(chunk, unit), :] = partial[u * unit : (u + 1) * unit, :]
    half = sent_refs[1].shape[0]
    for b in range(4 * quarter // LANES):
        line = jnp.sum(staged[b * LANES : (b + 1) * LANES, :].T, axis=0, keepdims=True)
        counts_ref[b : b + 1, :] = line
        sent_refs[0][half + b : half + b + 1, :] = line
    store_moments(plan, table, plan.units // 2, moments, sent_refs[::-1])


def own_kernel(plan, table, own_ref, stack_ref, first_ref, second_ref, moments):
    count, width = stack_ref.shape[0], stack_ref.shape[1] // 3
    block = min(BLOCK, count)
    for first in range(0, count, block):
        here = slice(first, first + block)
        added = jnp.dot(own_ref[:, here], stack_ref[here, width:], preferred_element_type=F32)
        if first == 0:
            moments[...] = added
        else:
            moments[...] += added
    store_moments(plan, table, 0, moments, (second_ref, first_ref))


def call(kernel, plan, table, operands, shapes, scratch, flops, vmem_mib, space=pltpu.VMEM):
    vmem = pl.BlockSpec(memory_space=pltpu.VMEM)
    moved = sum(math.prod(o.shape) * o.dtype.itemsize for o in operands)
    return pl.pallas_call(
        functools.partial(kernel, plan),
        in_specs=[pl.BlockSpec(memory_space=pltpu.SMEM)] + [pl.BlockSpec(memory_space=space)] * len(operands),
        out_specs=[vmem] * len(shapes),
        out_shape=[jax.ShapeDtypeStruct(*s) for s in shapes],
        scratch_shapes=[pltpu.VMEM(*s) if isinstance(s, tuple) else s for s in scratch],
        compiler_params=pltpu.CompilerParams(vmem_limit_bytes=vmem_mib * 2**20),
        cost_estimate=pl.CostEstimate(flops=flops, bytes_accessed=2 * moved, transcendentals=0),
    )(table, *operands)


def prepare(plan, table, features, logits, means, variances):
    count, width = features.shape
    comps = math.prod(logits.shape)
    *held, stack, log_weights = call(
        prepare_kernel,
        plan,
        table,
        [pltpu.with_memory_space_constraint(a, pltpu.HBM) for a in (features, logits, means, variances)],
        [(means.shape, F32)] * 2 + [((count, 3 * width), BF16), ((comps, LANES), F32)],
        [((count, width), BF16), (logits.shape, F32), pltpu.SemaphoreType.DMA((4,))],
        8 * count * width,
        16,
        pltpu.HBM,
    )
    return held, stack, log_weights


def early_scores(plan, table, means, variances, log_weights, stack):
    count, width = stack.shape[0], stack.shape[1] // 3
    comps = sum(m.shape[0] for m in means)
    return call(
        early_kernel,
        plan,
        table,
        [*means, *variances, log_weights, stack],
        [((comps, count), F32)],
        [((comps, 5 * width), BF16), ((comps, LANES), F32)],
        10 * comps * count * width,
        24,
    )[0]


def mixture(plan, table, means, variances, log_weights, stack, early):
    count, width = stack.shape[0], stack.shape[1] // 3
    half = sum(m.shape[0] for m in means)
    rows = half * (width // LANES)
    *sent, counts, row_scores, own = call(
        late_kernel,
        plan,
        table,
        [*means, *variances, log_weights, stack, early],
        [
            ((rows + COUNT_ROWS, LANES), F32),
            ((rows, LANES), F32),
            ((COUNT_ROWS, LANES), F32),
            ((1, count), F32),
            ((half, count), BF16),
        ],
        [
            ((half, 5 * width), BF16),
            ((half, LANES), F32),
            ((half, 2 * width), F32),
            ((2 * half, LANES), F32),
            ((2 * half, LANES), F32),
        ],
        16 * half * count * width,
        32,
    )
    kept = call(
        own_kernel,
        plan,
        table,
        [own, stack],
        [((rows, LANES), F32)] * 2,
        [((half, 2 * width), F32)],
        4 * half * count * width,
        16,
    )
    return sent, kept, counts, row_scores


def update_kernel(plan, pieces, total_rows, table, *refs):
    first_refs, second_refs = refs[:pieces], refs[pieces : 2 * pieces]
    counts_ref = refs[2 * pieces]
    means_ref, variances_ref, log_weights_ref, staged = refs[2 * pieces + 1 :]
    comps, width = means_ref.shape
    unit = plan.unit
    parts = width // LANES
    denominator = counts_ref[...] + 1.0
    log_weights_ref[...] = jnp.log(denominator / total_rows)
    inverse = 1.0 / denominator
    for b in range(comps // LANES):
        staged[b * LANES : (b + 1) * LANES, :] = columns(inverse[b : b + 1, :], LANES)
    for stream, stream_refs in enumerate((first_refs, second_refs)):
        slot = 0
        for ref in stream_refs:
            for first in range(0, ref.shape[0], unit * parts):
                chunk = pl.ds(pl.multiple_of(table[3 + stream, slot] * unit, unit), unit)
                scale = staged[chunk, :]
                for part in range(parts):
                    lanes = slice(part * LANES, (part + 1) * LANES)
                    moment = ref[first + part * unit : first + (part + 1) * unit, :]
                    if stream == 0:
                        means_ref[chunk, lanes] = moment * scale
                    else:
                        mean = means_ref[chunk, lanes]
                        variances_ref[chunk, lanes] = (moment + 1.0) * scale - mean * mean + 0.01
                slot += 1


def update(plan, table, first, second, counts, comps, width, total_rows):
    vmem = pl.BlockSpec(memory_space=pltpu.VMEM)
    shapes = [(comps, width), (comps, width), counts.shape]
    return pl.pallas_call(
        functools.partial(update_kernel, plan, len(first), total_rows),
        in_specs=[pl.BlockSpec(memory_space=pltpu.SMEM)] + [vmem] * (2 * len(first) + 1),
        out_specs=[vmem] * 3,
        scratch_shapes=[pltpu.VMEM((comps, LANES), F32)],
        out_shape=[jax.ShapeDtypeStruct(s, F32) for s in shapes],
        compiler_params=pltpu.CompilerParams(vmem_limit_bytes=16 * 2**20),
        cost_estimate=pl.CostEstimate(flops=8 * comps * width, bytes_accessed=16 * comps * width, transcendentals=0),
    )(table, *first, *second, counts)


def double(plan, held, step, arrived=None):
    arrived = [plan.swap(h, at) for h, at in zip(held, step)] if arrived is None else arrived
    return [jnp.concatenate(pair, axis=0) for pair in zip(held, arrived)]


def scatter(plan, sent, kept, counts):
    rows = kept[1].shape[0]
    for at, step in enumerate(zip(*plan.halving)):
        if at:
            rows //= 2
            sent = [jnp.concatenate([kept[0][rows:], counts], axis=0), kept[1][rows:]]
            kept = [k[:rows] for k in kept]
        arrived = [plan.swap(s, pair) for s, pair in zip(sent, step)]
        counts = counts + arrived[0][rows:]
        kept = [k + a[:rows] for k, a in zip(kept, arrived)]
    for pair in plan.whole:
        arrived = [plan.swap(jnp.concatenate([kept[0], counts], axis=0), pair), plan.swap(kept[1], pair)]
        counts = counts + arrived[0][rows:]
        kept = [k + a[:rows] for k, a in zip(kept, arrived)]
    return kept, 0.5 * (counts + plan.swap(counts, (0, 0)))


def on_device(plan, features, means, variances, weight_logits):
    comps = weight_logits.shape[0]
    width = means.shape[1]
    me = lax.axis_index(("grp", "comp"))
    table = lax.dynamic_index_in_dim(jnp.asarray(plan.tables), me, 0, keepdims=False)
    logits = weight_logits.reshape(comps // LANES, LANES)

    with jax.named_scope("gather_parameters"):
        arrived = [plan.swap(h, plan.gather[0]) for h in (means, variances)]
        held, stack, log_weights = prepare(plan, table, features, logits, means, variances)
        arrived, held, stack, log_weights, table = lax.optimization_barrier(
            (arrived, held, stack, log_weights, table)
        )
        held = double(plan, held, None, arrived)
        for step in plan.gather[1:-1]:
            held = double(plan, held, (step, step))
        last = [plan.swap(h, plan.gather[-1]) for h in held]
        pairs = [(h, plan.swap(h, (0, 0))) for h in held]
        early = early_scores(plan, table, *pairs, log_weights, stack)
        last, early = lax.optimization_barrier((last, early))
        pairs = [(l, plan.swap(l, (0, 0))) for l in last]
    sent, kept, counts, row_scores = mixture(plan, table, *pairs, log_weights, stack, early)
    with jax.named_scope("scatter_moments"):
        kept, counts = scatter(plan, sent, kept, counts)
    with jax.named_scope("gather_moments"):
        steps = list(zip(*plan.halving))[:0:-1]
        held = kept
        for step in steps[:-1]:
            held = double(plan, held, step)
        last = [plan.swap(h, at) for h, at in zip(held, steps[-1])]
        mates = [plan.swap(h, (0, 0)) for h in held]
        first, second = [[h, l, m, plan.swap(l, (0, 0))] for h, l, m in zip(held, last, mates)]

    total_rows = float(features.shape[0] * plan.devices + comps)
    fresh_means, fresh_variances, fresh_weights = update(
        plan, table, first, second, counts, comps, width, total_rows
    )
    return fresh_means, fresh_variances, fresh_weights.reshape(comps), row_scores.reshape(-1)


def solution(mesh):
    def whole(features, means, variances, weight_logits):
        plan = Plan(mesh.shape["grp"], mesh.shape["comp"], weight_logits.shape[0])
        return jax.shard_map(
            functools.partial(on_device, plan),
            mesh=mesh,
            in_specs=(P(("grp", "comp"), None), P("comp", None), P("comp", None), P()),
            out_specs=(P(), P(), P(), P(("grp", "comp"))),
            check_vma=False,
        )(features, means, variances, weight_logits)

    return whole
```

```python
import functools
import math

import jax
import jax.numpy as jnp
import numpy as np
from jax import lax
from jax.experimental import pallas as pl
from jax.experimental.pallas import tpu as pltpu
from jax.sharding import PartitionSpec as P

F32 = jnp.float32
BF16 = jnp.bfloat16
LANES = 128
COUNT_ROWS = 8
LOG2E = math.log2(math.e)
LN2 = math.log(2.0)
BLOCK = 1024


class Plan:
    def __init__(self, groups, owners, comps):
        self.devices = groups * owners
        self.owners = owners
        owner_bits = owners.bit_length() - 1
        group_bits = groups.bit_length() - 1
        assert owners == 1 << owner_bits and groups == 1 << group_bits and owner_bits >= 4
        piece = comps // owners
        group = list(range(owner_bits, owner_bits + group_bits))
        split = [1] + group[:1] + list(range(2, owner_bits - 1))
        while comps >> (len(split) + 1) < 16:
            split.pop()
        rest = [b for b in range(1, owner_bits + group_bits) if b not in split]
        self.units = 1 << (len(split) + 1)
        self.unit = comps // self.units
        assert piece % self.unit == 0
        per = piece // self.unit
        first, second, third, *others = split
        orders = (
            ((third, first, second), (second, third, first)),
            ((first, third, second), (second, first, third)),
        )
        self.halving = [
            [(0, 0)] + list(zip(zero, one)) + [(b, b) for b in others] for zero, one in orders
        ]
        self.whole = [(b, b) for b in rest]
        down = list(range(owner_bits - 1, 0, -1))
        self.gather = list(zip(down, down[:-2] + [down[-1], down[-2]]))

        def reach(device, steps, place):
            for t in reversed(range(len(steps))):
                if place >> t & 1:
                    device ^= 1 << steps[t][device & 1]
            return device

        n = range(self.devices)
        places = range(owners)
        gather_at = np.array([[reach(d, self.gather + [(0, 0)], p) % owners for p in places] for d in n])
        unit_chunk = (gather_at[:, :, None] * per + np.arange(per)).reshape(self.devices, self.units)
        owned = sorted([0] + split)
        slot_chunk = []
        for halving in self.halving:
            at = np.array([[reach(d, halving[::-1], j) for j in range(self.units)] for d in n])
            slot_chunk.append(sum((at >> b & 1) << i for i, b in enumerate(owned)))
        unit_slot = [np.take_along_axis(np.argsort(c, axis=1), unit_chunk, axis=1) for c in slot_chunk]
        self.tables = np.stack([unit_chunk, *unit_slot, *slot_chunk], axis=1).astype(np.int32)

    def swap(self, value, step):
        pairs = [(d, d ^ (1 << step[d & 1])) for d in range(self.devices)]
        return lax.ppermute(value, ("grp", "comp"), pairs)


def columns(row, height):
    return jnp.broadcast_to(row, (height, LANES)).T


def prepare_kernel(plan, table, *refs):
    sources, copies, (stack_ref, staged, features_ref, logits_ref, sems) = refs[:4], refs[4:6], refs[6:]
    targets = (features_ref, logits_ref, *copies)
    moves = [pltpu.make_async_copy(s, t, sems.at[i]) for i, (s, t) in enumerate(zip(sources, targets))]
    for move in moves:
        move.start()
    for move in moves:
        move.wait()
    logits = logits_ref[...]
    shifted = logits - jnp.max(logits)
    log_weights = shifted - jnp.log(jnp.sum(jnp.exp(shifted)))
    for b in range(logits.shape[0]):
        staged[b * LANES : (b + 1) * LANES, :] = columns(log_weights[b : b + 1, :], LANES)
    width = features_ref.shape[1]
    rows = features_ref[...]
    values = rows.astype(F32)
    squares = values * values
    high = squares.astype(BF16)
    stack_ref[:, :width] = (squares - high.astype(F32)).astype(BF16)
    stack_ref[:, width : 2 * width] = high
    stack_ref[:, 2 * width :] = rows


def build_weights(unit, table, first_units, mean_refs, variance_refs, log_weights, weights, offsets):
    at = 0
    width = mean_refs[0].shape[1]
    for mean_ref, variance_ref, first_unit in zip(mean_refs, variance_refs, first_units):
        for first in range(0, mean_ref.shape[0], unit):
            here = slice(at, at + unit)
            mean = mean_ref[first : first + unit, :]
            variance = variance_ref[first : first + unit, :]
            inverse = 1.0 / variance
            linear = mean * inverse
            constant = jnp.sum(jnp.log(variance) + mean * linear, axis=1, keepdims=True)
            chunk = pl.multiple_of(table[0, first_unit + first // unit] * unit, unit)
            log_weight = log_weights[pl.ds(chunk, unit), :]
            offsets[here, :] = (
                log_weight - 0.5 * constant - 0.5 * width * math.log(2.0 * math.pi)
            ) * LOG2E
            square = inverse * (-0.5 * LOG2E)
            linear = linear * LOG2E
            square_high = square.astype(BF16)
            linear_high = linear.astype(BF16)
            weights[here, :width] = square_high
            weights[here, width : 2 * width] = square_high
            weights[here, 2 * width : 3 * width] = linear_high
            weights[here, 3 * width : 4 * width] = (square - square_high.astype(F32)).astype(BF16)
            weights[here, 4 * width :] = (linear - linear_high.astype(F32)).astype(BF16)
            at += unit


def block_scores(stack, weights, offsets):
    width = stack.shape[1] // 3
    scores = lax.dot_general(
        weights[...],
        jnp.concatenate([stack, stack[:, width:]], axis=1),
        (((1,), (1,)), ((), ())),
        preferred_element_type=F32,
    )
    return scores + jnp.tile(offsets[...], (1, stack.shape[0] // LANES))


def store_moments(plan, table, first_unit, moments, targets):
    unit = plan.unit
    width = moments.shape[1] // 2
    parts = width // LANES
    for u in range(moments.shape[0] // unit):
        for column, target in enumerate(targets):
            slot = table[2 - column, first_unit + u] % (plan.units // 2)
            first = pl.multiple_of(slot * (unit * parts), unit)
            for part in range(parts):
                at = column * width + part * LANES
                target[pl.ds(first + part * unit, unit), :] = moments[
                    u * unit : (u + 1) * unit, at : at + LANES
                ]


def early_kernel(plan, first_units, table, *refs):
    pieces = len(first_units)
    mean_refs, variance_refs = refs[:pieces], refs[pieces : 2 * pieces]
    log_weights, stack_ref, powers_ref, highest_ref, totals_ref, weights, offsets = refs[2 * pieces :]
    count = stack_ref.shape[0]
    block = min(BLOCK, count)
    build_weights(plan.unit, table, first_units, mean_refs, variance_refs, log_weights, weights, offsets)
    for first in range(0, count, block):
        here = slice(first, first + block)
        scores = block_scores(stack_ref[here, :], weights, offsets)
        highest = jnp.max(scores, axis=0, keepdims=True)
        powers = jnp.exp2(scores - highest)
        powers_ref[:, here] = powers
        highest_ref[:, here] = highest
        totals_ref[:, here] = jnp.sum(powers, axis=0, keepdims=True)


def late_kernel(plan, table, *refs):
    mean_ref, variance_ref, log_weights, stack_ref = refs[:4]
    (powers_1, highest_1, totals_1), (powers_2, highest_2, totals_2) = refs[4:7], refs[7:10]
    sent_refs, counts_ref, scores_ref, own_ref = refs[10:12], refs[12], refs[13], refs[14]
    weights, offsets, moments, partial, staged = refs[15:]
    count, width = stack_ref.shape[0], stack_ref.shape[1] // 3
    block = min(2 * BLOCK, count)
    quarter = weights.shape[0]
    firsts = (3 * plan.units // 4,)
    build_weights(plan.unit, table, firsts, (mean_ref,), (variance_ref,), log_weights, weights, offsets)
    for first in range(0, count, block):
        here = slice(first, first + block)
        stack = stack_ref[here, :]
        scores = block_scores(stack, weights, offsets)
        highest = jnp.maximum(
            jnp.maximum(highest_1[:, here], highest_2[:, here]), jnp.max(scores, axis=0, keepdims=True)
        )
        scale_1 = jnp.exp2(highest_1[:, here] - highest)
        scale_2 = jnp.exp2(highest_2[:, here] - highest)
        powers = jnp.exp2(scores - highest)
        totals = (
            totals_1[:, here] * scale_1
            + totals_2[:, here] * scale_2
            + jnp.sum(powers, axis=0, keepdims=True)
        )
        scores_ref[:, here] = (highest + jnp.log2(totals)) * (LN2 / width)
        inverse = 1.0 / totals
        scale_1 = scale_1 * inverse
        scale_2 = scale_2 * inverse
        parts = (
            (powers_1[:quarter, here] * scale_1).astype(BF16),
            (powers_2[:, here] * scale_2).astype(BF16),
            (powers_1[quarter:, here] * scale_1).astype(BF16),
            (powers * inverse).astype(BF16),
        )
        own_ref[:quarter, here] = parts[0]
        own_ref[quarter:, here] = parts[1]
        added = jnp.dot(
            jnp.concatenate(parts[2:], axis=0),
            stack[:, width:],
            preferred_element_type=F32,
        )
        if first == 0:
            moments[...] = added
        else:
            moments[...] += added
        for at, part in enumerate(parts):
            rounded = part.astype(F32)
            counted = rounded[:, :LANES]
            for b in range(1, block // LANES):
                counted = counted + rounded[:, b * LANES : (b + 1) * LANES]
            here = slice(at * quarter, (at + 1) * quarter)
            if first == 0:
                partial[here, :] = counted
            else:
                partial[here, :] += counted

    unit = plan.unit
    for u in range(plan.units):
        chunk = pl.multiple_of(table[0, u] * unit, unit)
        staged[pl.ds(chunk, unit), :] = partial[u * unit : (u + 1) * unit, :]
    half = sent_refs[1].shape[0]
    for b in range(4 * quarter // LANES):
        line = jnp.sum(staged[b * LANES : (b + 1) * LANES, :].T, axis=0, keepdims=True)
        counts_ref[b : b + 1, :] = line
        sent_refs[0][half + b : half + b + 1, :] = line
    store_moments(plan, table, plan.units // 2, moments, sent_refs[::-1])


def own_kernel(plan, table, own_ref, stack_ref, first_ref, second_ref, moments):
    count, width = stack_ref.shape[0], stack_ref.shape[1] // 3
    block = min(BLOCK, count)
    for first in range(0, count, block):
        here = slice(first, first + block)
        added = jnp.dot(own_ref[:, here], stack_ref[here, width:], preferred_element_type=F32)
        if first == 0:
            moments[...] = added
        else:
            moments[...] += added
    store_moments(plan, table, 0, moments, (second_ref, first_ref))


def call(kernel, plan, table, operands, shapes, scratch, flops, vmem_mib, space=pltpu.VMEM):
    vmem = pl.BlockSpec(memory_space=pltpu.VMEM)
    moved = sum(math.prod(o.shape) * o.dtype.itemsize for o in operands)
    return pl.pallas_call(
        functools.partial(kernel, plan),
        in_specs=[pl.BlockSpec(memory_space=pltpu.SMEM)] + [pl.BlockSpec(memory_space=space)] * len(operands),
        out_specs=[vmem] * len(shapes),
        out_shape=[jax.ShapeDtypeStruct(*s) for s in shapes],
        scratch_shapes=[pltpu.VMEM(*s) if isinstance(s, tuple) else s for s in scratch],
        compiler_params=pltpu.CompilerParams(vmem_limit_bytes=vmem_mib * 2**20),
        cost_estimate=pl.CostEstimate(flops=flops, bytes_accessed=2 * moved, transcendentals=0),
    )(table, *operands)


def prepare(plan, table, features, logits, means, variances):
    count, width = features.shape
    comps = math.prod(logits.shape)
    *held, stack, log_weights = call(
        prepare_kernel,
        plan,
        table,
        [pltpu.with_memory_space_constraint(a, pltpu.HBM) for a in (features, logits, means, variances)],
        [(means.shape, F32)] * 2 + [((count, 3 * width), BF16), ((comps, LANES), F32)],
        [((count, width), BF16), (logits.shape, F32), pltpu.SemaphoreType.DMA((4,))],
        8 * count * width,
        16,
        pltpu.HBM,
    )
    return held, stack, log_weights


def early_scores(plan, table, first_units, means, variances, log_weights, stack):
    count, width = stack.shape[0], stack.shape[1] // 3
    comps = sum(m.shape[0] for m in means)
    return call(
        lambda plan, *refs: early_kernel(plan, first_units, *refs),
        plan,
        table,
        [*means, *variances, log_weights, stack],
        [((comps, count), F32), ((1, count), F32), ((1, count), F32)],
        [((comps, 5 * width), BF16), ((comps, LANES), F32)],
        10 * comps * count * width,
        24,
    )


def mixture(plan, table, mean, variance, log_weights, stack, early):
    count, width = stack.shape[0], stack.shape[1] // 3
    half = 2 * mean.shape[0]
    rows = half * (width // LANES)
    *sent, counts, row_scores, own = call(
        late_kernel,
        plan,
        table,
        [mean, variance, log_weights, stack, *early],
        [
            ((rows + COUNT_ROWS, LANES), F32),
            ((rows, LANES), F32),
            ((COUNT_ROWS, LANES), F32),
            ((1, count), F32),
            ((half, count), BF16),
        ],
        [
            ((half // 2, 5 * width), BF16),
            ((half // 2, LANES), F32),
            ((half, 2 * width), F32),
            ((2 * half, LANES), F32),
            ((2 * half, LANES), F32),
        ],
        9 * half * count * width,
        32,
    )
    kept = call(
        own_kernel,
        plan,
        table,
        [own, stack],
        [((rows, LANES), F32)] * 2,
        [((half, 2 * width), F32)],
        4 * half * count * width,
        16,
    )
    return sent, kept, counts, row_scores


def update_kernel(plan, pieces, total_rows, table, *refs):
    first_refs, second_refs = refs[:pieces], refs[pieces : 2 * pieces]
    counts_ref = refs[2 * pieces]
    means_ref, variances_ref, log_weights_ref, staged = refs[2 * pieces + 1 :]
    comps, width = means_ref.shape
    unit = plan.unit
    parts = width // LANES
    denominator = counts_ref[...] + 1.0
    log_weights_ref[...] = jnp.log(denominator / total_rows)
    inverse = 1.0 / denominator
    for b in range(comps // LANES):
        staged[b * LANES : (b + 1) * LANES, :] = columns(inverse[b : b + 1, :], LANES)
    for stream, stream_refs in enumerate((first_refs, second_refs)):
        slot = 0
        for ref in stream_refs:
            for first in range(0, ref.shape[0], unit * parts):
                chunk = pl.ds(pl.multiple_of(table[3 + stream, slot] * unit, unit), unit)
                scale = staged[chunk, :]
                for part in range(parts):
                    lanes = slice(part * LANES, (part + 1) * LANES)
                    moment = ref[first + part * unit : first + (part + 1) * unit, :]
                    if stream == 0:
                        means_ref[chunk, lanes] = moment * scale
                    else:
                        mean = means_ref[chunk, lanes]
                        variances_ref[chunk, lanes] = (moment + 1.0) * scale - mean * mean + 0.01
                slot += 1


def update(plan, table, first, second, counts, comps, width, total_rows):
    vmem = pl.BlockSpec(memory_space=pltpu.VMEM)
    shapes = [(comps, width), (comps, width), counts.shape]
    return pl.pallas_call(
        functools.partial(update_kernel, plan, len(first), total_rows),
        in_specs=[pl.BlockSpec(memory_space=pltpu.SMEM)] + [vmem] * (2 * len(first) + 1),
        out_specs=[vmem] * 3,
        scratch_shapes=[pltpu.VMEM((comps, LANES), F32)],
        out_shape=[jax.ShapeDtypeStruct(s, F32) for s in shapes],
        compiler_params=pltpu.CompilerParams(vmem_limit_bytes=16 * 2**20),
        cost_estimate=pl.CostEstimate(flops=8 * comps * width, bytes_accessed=16 * comps * width, transcendentals=0),
    )(table, *first, *second, counts)


def double(plan, held, step, arrived=None):
    arrived = [plan.swap(h, at) for h, at in zip(held, step)] if arrived is None else arrived
    return [jnp.concatenate(pair, axis=0) for pair in zip(held, arrived)]


def scatter(plan, sent, kept, counts):
    rows = kept[1].shape[0]
    for at, step in enumerate(zip(*plan.halving)):
        if at:
            rows //= 2
            sent = [jnp.concatenate([kept[0][rows:], counts], axis=0), kept[1][rows:]]
            kept = [k[:rows] for k in kept]
        arrived = [plan.swap(s, pair) for s, pair in zip(sent, step)]
        counts = counts + arrived[0][rows:]
        kept = [k + a[:rows] for k, a in zip(kept, arrived)]
    for pair in plan.whole:
        arrived = [plan.swap(jnp.concatenate([kept[0], counts], axis=0), pair), plan.swap(kept[1], pair)]
        counts = counts + arrived[0][rows:]
        kept = [k + a[:rows] for k, a in zip(kept, arrived)]
    return kept, 0.5 * (counts + plan.swap(counts, (0, 0)))


def on_device(plan, features, means, variances, weight_logits):
    comps = weight_logits.shape[0]
    width = means.shape[1]
    me = lax.axis_index(("grp", "comp"))
    table = lax.dynamic_index_in_dim(jnp.asarray(plan.tables), me, 0, keepdims=False)
    logits = weight_logits.reshape(comps // LANES, LANES)

    with jax.named_scope("gather_parameters"):
        arrived = [plan.swap(h, plan.gather[0]) for h in (means, variances)]
        held, stack, log_weights = prepare(plan, table, features, logits, means, variances)
        arrived, held, stack, log_weights, table = lax.optimization_barrier(
            (arrived, held, stack, log_weights, table)
        )
        held = double(plan, held, None, arrived)
        for step in plan.gather[1:-1]:
            held = double(plan, held, (step, step))
        last = [plan.swap(h, plan.gather[-1]) for h in held]
        pairs = [(h, plan.swap(h, (0, 0))) for h in held]
        firsts = (0, plan.units // 2)
        early = early_scores(plan, table, firsts, *pairs, log_weights, stack)
        last, early = lax.optimization_barrier((last, early))
        mates = [plan.swap(l, (0, 0)) for l in last]
        firsts = (plan.units // 4,)
        early += early_scores(plan, table, firsts, last[:1], last[1:], log_weights, stack)
    sent, kept, counts, row_scores = mixture(plan, table, *mates, log_weights, stack, early)
    with jax.named_scope("scatter_moments"):
        kept, counts = scatter(plan, sent, kept, counts)
    with jax.named_scope("gather_moments"):
        steps = list(zip(*plan.halving))[:0:-1]
        held = kept
        for step in steps[:-1]:
            held = double(plan, held, step)
        last = [plan.swap(h, at) for h, at in zip(held, steps[-1])]
        mates = [plan.swap(h, (0, 0)) for h in held]
        first, second = [[h, l, m, plan.swap(l, (0, 0))] for h, l, m in zip(held, last, mates)]

    total_rows = float(features.shape[0] * plan.devices + comps)
    fresh_means, fresh_variances, fresh_weights = update(
        plan, table, first, second, counts, comps, width, total_rows
    )
    return fresh_means, fresh_variances, fresh_weights.reshape(comps), row_scores.reshape(-1)


def solution(mesh):
    def whole(features, means, variances, weight_logits):
        plan = Plan(mesh.shape["grp"], mesh.shape["comp"], weight_logits.shape[0])
        return jax.shard_map(
            functools.partial(on_device, plan),
            mesh=mesh,
            in_specs=(P(("grp", "comp"), None), P("comp", None), P("comp", None), P()),
            out_specs=(P(), P(), P(), P(("grp", "comp"))),
            check_vma=False,
        )(features, means, variances, weight_logits)

    return whole
```

```python
import functools
import math

import jax
import jax.numpy as jnp
import numpy as np
from jax import lax
from jax.experimental import pallas as pl
from jax.experimental.pallas import tpu as pltpu
from jax.sharding import PartitionSpec as P

F32 = jnp.float32
BF16 = jnp.bfloat16
LANES = 128
COUNT_ROWS = 8
LOG2E = math.log2(math.e)
LN2 = math.log(2.0)
BLOCK = 1024


class Plan:
    def __init__(self, groups, owners, comps):
        self.devices = groups * owners
        self.owners = owners
        owner_bits = owners.bit_length() - 1
        group_bits = groups.bit_length() - 1
        assert owners == 1 << owner_bits and groups == 1 << group_bits
        assert owner_bits >= 4 and group_bits >= 1 and comps % owners == 0
        self.units = owners
        self.unit = comps // owners
        self.masks = [1] + [1 << b | 1 for b in range(1, owner_bits)]
        self.masks += [1 << b for b in range(owner_bits, owner_bits + group_bits)]
        split = [1, owner_bits] + list(range(2, owner_bits - 1))
        rest = [b for b in range(1, owner_bits + group_bits) if b not in split]
        first, second, third, *others = split
        orders = (
            ((third, first, second), (second, third, first)),
            ((first, second, third), (second, third, first)),
        )
        self.halving = [
            [(0, 0)] + list(zip(zero, one)) + [(b, b) for b in others] for zero, one in orders
        ]
        self.whole = [(b, b) for b in rest]
        down = list(range(owner_bits - 1, 0, -1))
        self.gather = list(zip(down, down[:-2] + [down[-1], down[-2]]))

        def reach(device, steps, place):
            for t in reversed(range(len(steps))):
                if place >> t & 1:
                    device = self.partner(device, steps[t])
            return device

        def chunk(device):
            place = sum((device >> b & 1) << i for i, b in enumerate(split)) << 1
            return place | (self.colour(place) ^ self.colour(device))

        n = range(self.devices)
        places = range(self.units)
        unit_chunk = np.array([[reach(d, self.gather + [(0, 0)], p) % owners for p in places] for d in n])
        slot_chunk = [
            np.array([[chunk(reach(d, halving[::-1], j)) for j in places] for d in n]) for halving in self.halving
        ]
        unit_slot = [np.take_along_axis(np.argsort(c, axis=1), unit_chunk, axis=1) for c in slot_chunk]
        self.tables = np.stack([unit_chunk, *unit_slot, *slot_chunk], axis=1).astype(np.int32)

    def colour(self, device):
        return (device % self.owners).bit_count() & 1

    def partner(self, device, step):
        return device ^ self.masks[step[self.colour(device)]]

    def swap(self, value, step):
        pairs = [(d, self.partner(d, step)) for d in range(self.devices)]
        return lax.ppermute(value, ("grp", "comp"), pairs)


def columns(row, height):
    return jnp.broadcast_to(row, (height, LANES)).T


def prepare_kernel(plan, table, *refs):
    sources, copies, (stack_ref, staged, features_ref, logits_ref, sems) = refs[:4], refs[4:6], refs[6:]
    targets = (features_ref, logits_ref, *copies)
    moves = [pltpu.make_async_copy(s, t, sems.at[i]) for i, (s, t) in enumerate(zip(sources, targets))]
    for move in moves:
        move.start()
    for move in moves:
        move.wait()
    logits = logits_ref[...]
    shifted = logits - jnp.max(logits)
    log_weights = shifted - jnp.log(jnp.sum(jnp.exp(shifted)))
    for b in range(logits.shape[0]):
        staged[b * LANES : (b + 1) * LANES, :] = columns(log_weights[b : b + 1, :], LANES)
    width = features_ref.shape[1]
    rows = features_ref[...]
    values = rows.astype(F32)
    squares = values * values
    high = squares.astype(BF16)
    stack_ref[:, :width] = (squares - high.astype(F32)).astype(BF16)
    stack_ref[:, width : 2 * width] = high
    stack_ref[:, 2 * width :] = rows


def build_weights(unit, table, first_units, mean_refs, variance_refs, log_weights, weights, offsets):
    at = 0
    width = mean_refs[0].shape[1]
    for mean_ref, variance_ref, first_unit in zip(mean_refs, variance_refs, first_units):
        for first in range(0, mean_ref.shape[0], unit):
            here = slice(at, at + unit)
            mean = mean_ref[first : first + unit, :]
            variance = variance_ref[first : first + unit, :]
            inverse = 1.0 / variance
            linear = mean * inverse
            constant = jnp.sum(jnp.log(variance) + mean * linear, axis=1, keepdims=True)
            chunk = pl.multiple_of(table[0, first_unit + first // unit] * unit, unit)
            log_weight = log_weights[pl.ds(chunk, unit), :]
            offsets[here, :] = (
                log_weight - 0.5 * constant - 0.5 * width * math.log(2.0 * math.pi)
            ) * LOG2E
            square = inverse * (-0.5 * LOG2E)
            linear = linear * LOG2E
            square_high = square.astype(BF16)
            linear_high = linear.astype(BF16)
            weights[here, :width] = square_high
            weights[here, width : 2 * width] = square_high
            weights[here, 2 * width : 3 * width] = linear_high
            weights[here, 3 * width : 4 * width] = (square - square_high.astype(F32)).astype(BF16)
            weights[here, 4 * width :] = (linear - linear_high.astype(F32)).astype(BF16)
            at += unit


def block_scores(stack, weights, offsets):
    width = stack.shape[1] // 3
    scores = lax.dot_general(
        weights[...],
        jnp.concatenate([stack, stack[:, width:]], axis=1),
        (((1,), (1,)), ((), ())),
        preferred_element_type=F32,
    )
    return scores + jnp.tile(offsets[...], (1, stack.shape[0] // LANES))


def store_moments(plan, table, first_unit, moments, targets):
    unit = plan.unit
    width = moments.shape[1] // 2
    parts = width // LANES
    for u in range(moments.shape[0] // unit):
        for column, target in enumerate(targets):
            slot = table[2 - column, first_unit + u] % (plan.units // 2)
            first = pl.multiple_of(slot * (unit * parts), unit)
            for part in range(parts):
                at = column * width + part * LANES
                target[pl.ds(first + part * unit, unit), :] = moments[
                    u * unit : (u + 1) * unit, at : at + LANES
                ]


def early_kernel(plan, first_units, table, *refs):
    pieces = len(first_units)
    mean_refs, variance_refs = refs[:pieces], refs[pieces : 2 * pieces]
    log_weights, stack_ref, powers_ref, highest_ref, totals_ref, weights, offsets = refs[2 * pieces :]
    count = stack_ref.shape[0]
    block = min(BLOCK, count)
    build_weights(plan.unit, table, first_units, mean_refs, variance_refs, log_weights, weights, offsets)
    for first in range(0, count, block):
        here = slice(first, first + block)
        scores = block_scores(stack_ref[here, :], weights, offsets)
        highest = jnp.max(scores, axis=0, keepdims=True)
        powers = jnp.exp2(scores - highest)
        powers_ref[:, here] = powers
        highest_ref[:, here] = highest
        totals_ref[:, here] = jnp.sum(powers, axis=0, keepdims=True)


def late_kernel(plan, table, *refs):
    mean_ref, variance_ref, log_weights, stack_ref = refs[:4]
    (powers_1, highest_1, totals_1), (powers_2, highest_2, totals_2) = refs[4:7], refs[7:10]
    sent_refs, counts_ref, scores_ref, own_ref = refs[10:12], refs[12], refs[13], refs[14]
    weights, offsets, moments, partial, staged = refs[15:]
    count, width = stack_ref.shape[0], stack_ref.shape[1] // 3
    block = min(2 * BLOCK, count)
    quarter = weights.shape[0]
    firsts = (3 * plan.units // 4,)
    build_weights(plan.unit, table, firsts, (mean_ref,), (variance_ref,), log_weights, weights, offsets)
    for first in range(0, count, block):
        here = slice(first, first + block)
        stack = stack_ref[here, :]
        scores = block_scores(stack, weights, offsets)
        highest = jnp.maximum(
            jnp.maximum(highest_1[:, here], highest_2[:, here]), jnp.max(scores, axis=0, keepdims=True)
        )
        scale_1 = jnp.exp2(highest_1[:, here] - highest)
        scale_2 = jnp.exp2(highest_2[:, here] - highest)
        powers = jnp.exp2(scores - highest)
        totals = (
            totals_1[:, here] * scale_1
            + totals_2[:, here] * scale_2
            + jnp.sum(powers, axis=0, keepdims=True)
        )
        scores_ref[:, here] = (highest + jnp.log2(totals)) * (LN2 / width)
        inverse = 1.0 / totals
        scale_1 = scale_1 * inverse
        scale_2 = scale_2 * inverse
        parts = (
            (powers_1[:quarter, here] * scale_1).astype(BF16),
            (powers_2[:, here] * scale_2).astype(BF16),
            (powers_1[quarter:, here] * scale_1).astype(BF16),
            (powers * inverse).astype(BF16),
        )
        own_ref[:quarter, here] = parts[0]
        own_ref[quarter:, here] = parts[1]
        added = jnp.dot(
            jnp.concatenate(parts[2:], axis=0),
            stack[:, width:],
            preferred_element_type=F32,
        )
        if first == 0:
            moments[...] = added
        else:
            moments[...] += added
        for at, part in enumerate(parts):
            rounded = part.astype(F32)
            counted = rounded[:, :LANES]
            for b in range(1, block // LANES):
                counted = counted + rounded[:, b * LANES : (b + 1) * LANES]
            here = slice(at * quarter, (at + 1) * quarter)
            if first == 0:
                partial[here, :] = counted
            else:
                partial[here, :] += counted

    unit = plan.unit
    for u in range(plan.units):
        chunk = pl.multiple_of(table[0, u] * unit, unit)
        staged[pl.ds(chunk, unit), :] = partial[u * unit : (u + 1) * unit, :]
    half = sent_refs[1].shape[0]
    for b in range(4 * quarter // LANES):
        line = jnp.sum(staged[b * LANES : (b + 1) * LANES, :].T, axis=0, keepdims=True)
        counts_ref[b : b + 1, :] = line
        sent_refs[0][half + b : half + b + 1, :] = line
    store_moments(plan, table, plan.units // 2, moments, sent_refs[::-1])


def own_kernel(plan, table, own_ref, stack_ref, first_ref, second_ref, moments):
    count, width = stack_ref.shape[0], stack_ref.shape[1] // 3
    block = min(BLOCK, count)
    for first in range(0, count, block):
        here = slice(first, first + block)
        added = jnp.dot(own_ref[:, here], stack_ref[here, width:], preferred_element_type=F32)
        if first == 0:
            moments[...] = added
        else:
            moments[...] += added
    store_moments(plan, table, 0, moments, (second_ref, first_ref))


def call(kernel, plan, table, operands, shapes, scratch, flops, vmem_mib, space=pltpu.VMEM):
    vmem = pl.BlockSpec(memory_space=pltpu.VMEM)
    moved = sum(math.prod(o.shape) * o.dtype.itemsize for o in operands)
    return pl.pallas_call(
        functools.partial(kernel, plan),
        in_specs=[pl.BlockSpec(memory_space=pltpu.SMEM)] + [pl.BlockSpec(memory_space=space)] * len(operands),
        out_specs=[vmem] * len(shapes),
        out_shape=[jax.ShapeDtypeStruct(*s) for s in shapes],
        scratch_shapes=[pltpu.VMEM(*s) if isinstance(s, tuple) else s for s in scratch],
        compiler_params=pltpu.CompilerParams(vmem_limit_bytes=vmem_mib * 2**20),
        cost_estimate=pl.CostEstimate(flops=flops, bytes_accessed=2 * moved, transcendentals=0),
    )(table, *operands)


def prepare(plan, table, features, logits, means, variances):
    count, width = features.shape
    comps = math.prod(logits.shape)
    *held, stack, log_weights = call(
        prepare_kernel,
        plan,
        table,
        [pltpu.with_memory_space_constraint(a, pltpu.HBM) for a in (features, logits, means, variances)],
        [(means.shape, F32)] * 2 + [((count, 3 * width), BF16), ((comps, LANES), F32)],
        [((count, width), BF16), (logits.shape, F32), pltpu.SemaphoreType.DMA((4,))],
        8 * count * width,
        16,
        pltpu.HBM,
    )
    return held, stack, log_weights


def early_scores(plan, table, first_units, means, variances, log_weights, stack):
    count, width = stack.shape[0], stack.shape[1] // 3
    comps = sum(m.shape[0] for m in means)
    return call(
        lambda plan, *refs: early_kernel(plan, first_units, *refs),
        plan,
        table,
        [*means, *variances, log_weights, stack],
        [((comps, count), F32), ((1, count), F32), ((1, count), F32)],
        [((comps, 5 * width), BF16), ((comps, LANES), F32)],
        10 * comps * count * width,
        24,
    )


def mixture(plan, table, mean, variance, log_weights, stack, early):
    count, width = stack.shape[0], stack.shape[1] // 3
    half = 2 * mean.shape[0]
    rows = half * (width // LANES)
    *sent, counts, row_scores, own = call(
        late_kernel,
        plan,
        table,
        [mean, variance, log_weights, stack, *early],
        [
            ((rows + COUNT_ROWS, LANES), F32),
            ((rows, LANES), F32),
            ((COUNT_ROWS, LANES), F32),
            ((1, count), F32),
            ((half, count), BF16),
        ],
        [
            ((half // 2, 5 * width), BF16),
            ((half // 2, LANES), F32),
            ((half, 2 * width), F32),
            ((2 * half, LANES), F32),
            ((2 * half, LANES), F32),
        ],
        9 * half * count * width,
        32,
    )
    kept = call(
        own_kernel,
        plan,
        table,
        [own, stack],
        [((rows, LANES), F32)] * 2,
        [((half, 2 * width), F32)],
        4 * half * count * width,
        16,
    )
    return sent, kept, counts, row_scores


def scale_kernel(plan, total_rows, table, counts_ref, log_weights_ref, scale_ref):
    denominator = counts_ref[...] + 1.0
    log_weights_ref[...] = jnp.log(denominator / total_rows)
    inverse = 1.0 / denominator
    for b in range(counts_ref.shape[0]):
        scale_ref[b * LANES : (b + 1) * LANES, :] = columns(inverse[b : b + 1, :], LANES)


def update_kernel(plan, first_slot, table, *refs):
    piece_refs, scale_ref = (refs[:2], refs[2:4]), refs[4]
    means_ref, variances_ref, mean_buffer, variance_buffer, sems = refs[-5:]
    width = mean_buffer.shape[1]
    unit = plan.unit
    parts = width // LANES
    moves = []
    for stream, buffer, target in ((0, mean_buffer, means_ref), (1, variance_buffer, variances_ref)):
        slot = first_slot
        for ref in piece_refs[stream]:
            for first in range(0, ref.shape[0], unit * parts):
                chunk = pl.ds(pl.multiple_of(table[3 + stream, slot] * unit, unit), unit)
                scale = scale_ref[chunk, :]
                for part in range(parts):
                    lanes = slice(part * LANES, (part + 1) * LANES)
                    moment = ref[first + part * unit : first + (part + 1) * unit, :]
                    if stream == 0:
                        buffer[chunk, lanes] = moment * scale
                    else:
                        mean = mean_buffer[chunk, lanes]
                        buffer[chunk, lanes] = (moment + 1.0) * scale - mean * mean + 0.01
                sem = sems.at[stream, slot - first_slot]
                move = pltpu.make_async_copy(buffer.at[chunk, :], target.at[chunk, :], sem)
                move.start()
                moves.append(move)
                slot += 1
    for move in moves:
        move.wait()


def update(plan, table, first_slot, first, second, scale, shape, earlier=()):
    vmem = pl.BlockSpec(memory_space=pltpu.VMEM)
    hbm = pl.BlockSpec(memory_space=pl.ANY)
    operands = [*first, *second, scale]
    return pl.pallas_call(
        functools.partial(update_kernel, plan, first_slot),
        in_specs=[pl.BlockSpec(memory_space=pltpu.SMEM)] + [vmem] * len(operands) + [hbm] * len(earlier),
        out_specs=[hbm] * 2,
        out_shape=[jax.ShapeDtypeStruct(shape, F32)] * 2,
        scratch_shapes=[
            pltpu.VMEM(shape, F32),
            pltpu.VMEM(shape, F32),
            pltpu.SemaphoreType.DMA((2, plan.units // 2)),
        ],
        input_output_aliases={1 + len(operands) + i: i for i in range(len(earlier))},
        compiler_params=pltpu.CompilerParams(vmem_limit_bytes=16 * 2**20),
        cost_estimate=pl.CostEstimate(
            flops=4 * math.prod(shape), bytes_accessed=8 * math.prod(shape), transcendentals=0
        ),
    )(table, *operands, *earlier)


def double(plan, held, step, arrived=None):
    arrived = [plan.swap(h, at) for h, at in zip(held, step)] if arrived is None else arrived
    return [jnp.concatenate(pair, axis=0) for pair in zip(held, arrived)]


def scatter(plan, sent, kept, counts):
    rows = kept[1].shape[0]
    for at, step in enumerate(zip(*plan.halving)):
        if at:
            rows //= 2
            sent = [jnp.concatenate([kept[0][rows:], counts], axis=0), kept[1][rows:]]
            kept = [k[:rows] for k in kept]
        arrived = [plan.swap(s, pair) for s, pair in zip(sent, step)]
        counts = counts + arrived[0][rows:]
        kept = [k + a[:rows] for k, a in zip(kept, arrived)]
    for pair in plan.whole:
        arrived = [plan.swap(jnp.concatenate([kept[0], counts], axis=0), pair), plan.swap(kept[1], pair)]
        counts = counts + arrived[0][rows:]
        kept = [k + a[:rows] for k, a in zip(kept, arrived)]
    return kept, 0.5 * (counts + plan.swap(counts, (0, 0)))


def on_device(plan, features, means, variances, weight_logits):
    comps = weight_logits.shape[0]
    width = means.shape[1]
    me = lax.axis_index(("grp", "comp"))
    table = lax.dynamic_index_in_dim(jnp.asarray(plan.tables), me, 0, keepdims=False)
    logits = weight_logits.reshape(comps // LANES, LANES)

    with jax.named_scope("gather_parameters"):
        arrived = [plan.swap(h, plan.gather[0]) for h in (means, variances)]
        held, stack, log_weights = prepare(plan, table, features, logits, means, variances)
        arrived, held, stack, log_weights, table = lax.optimization_barrier(
            (arrived, held, stack, log_weights, table)
        )
        held = double(plan, held, None, arrived)
        for step in plan.gather[1:-1]:
            held = double(plan, held, (step, step))
        last = [plan.swap(h, plan.gather[-1]) for h in held]
        pairs = [(h, plan.swap(h, (0, 0))) for h in held]
        firsts = (0, plan.units // 2)
        early = early_scores(plan, table, firsts, *pairs, log_weights, stack)
        last, early = lax.optimization_barrier((last, early))
        mates = [plan.swap(l, (0, 0)) for l in last]
        firsts = (plan.units // 4,)
        early += early_scores(plan, table, firsts, last[:1], last[1:], log_weights, stack)
    sent, kept, counts, row_scores = mixture(plan, table, *mates, log_weights, stack, early)
    with jax.named_scope("scatter_moments"):
        kept, counts = scatter(plan, sent, kept, counts)
    with jax.named_scope("gather_moments"):
        total_rows = float(features.shape[0] * plan.devices + comps)
        log_weights, scale = call(
            lambda plan, *refs: scale_kernel(plan, total_rows, *refs),
            plan,
            table,
            [counts],
            [(counts.shape, F32), ((comps, LANES), F32)],
            [],
            comps,
            8,
        )
        steps = list(zip(*plan.halving))[:0:-1]
        held = kept
        for step in steps[:-1]:
            held = double(plan, held, step)
        last = [plan.swap(h, at) for h, at in zip(held, steps[-1])]
        mates = [plan.swap(h, (0, 0)) for h in held]
        last, scale = lax.optimization_barrier((last, scale))
        own = [[h, l] for h, l in zip(held, last)]
        others = [[m, plan.swap(l, (0, 0))] for m, l in zip(mates, last)]
    fresh = update(plan, table, 0, *own, scale, (comps, width))
    fresh_means, fresh_variances = update(
        plan, table, plan.units // 2, *others, scale, (comps, width), fresh
    )
    return fresh_means, fresh_variances, log_weights.reshape(comps), row_scores.reshape(-1)


def solution(mesh):
    def whole(features, means, variances, weight_logits):
        plan = Plan(mesh.shape["grp"], mesh.shape["comp"], weight_logits.shape[0])
        return jax.shard_map(
            functools.partial(on_device, plan),
            mesh=mesh,
            in_specs=(P(("grp", "comp"), None), P("comp", None), P("comp", None), P()),
            out_specs=(P(), P(), P(), P(("grp", "comp"))),
            check_vma=False,
        )(features, means, variances, weight_logits)

    return whole
```

```python
import functools
import math

import jax
import jax.numpy as jnp
import numpy as np
from jax import lax
from jax.experimental import pallas as pl
from jax.experimental.pallas import tpu as pltpu
from jax.sharding import PartitionSpec as P

F32 = jnp.float32
BF16 = jnp.bfloat16
LANES = 128
COUNT_ROWS = 8
LOG2E = math.log2(math.e)
LN2 = math.log(2.0)
BLOCK = 1024


class Plan:
    def __init__(self, groups, owners, comps):
        self.devices = groups * owners
        self.owners = owners
        owner_bits = owners.bit_length() - 1
        group_bits = groups.bit_length() - 1
        assert owners == 1 << owner_bits and groups == 1 << group_bits
        assert owner_bits >= 4 and group_bits >= 1 and comps % owners == 0
        self.units = owners
        self.unit = comps // owners
        self.masks = [1] + [1 << b | 1 for b in range(1, owner_bits)]
        self.masks += [1 << b for b in range(owner_bits, owner_bits + group_bits)]
        split = [1, owner_bits] + list(range(2, owner_bits - 1))
        rest = [b for b in range(1, owner_bits + group_bits) if b not in split]
        first, second, third, *others = split
        orders = (
            ((third, first, second), (second, third, first)),
            ((first, second, third), (second, third, first)),
        )
        self.halving = [
            [(0, 0)] + list(zip(zero, one)) + [(b, b) for b in others] for zero, one in orders
        ]
        self.whole = [(b, b) for b in rest]
        down = list(range(owner_bits - 1, 0, -1))
        self.gather = list(zip(down, down[:-2] + [down[-1], down[-2]]))

        def reach(device, steps, place):
            for t in reversed(range(len(steps))):
                if place >> t & 1:
                    device = self.partner(device, steps[t])
            return device

        def chunk(device):
            place = sum((device >> b & 1) << i for i, b in enumerate(split)) << 1
            return place | (self.colour(place) ^ self.colour(device))

        n = range(self.devices)
        places = range(self.units)
        unit_chunk = np.array([[reach(d, self.gather + [(0, 0)], p) % owners for p in places] for d in n])
        slot_chunk = [
            np.array([[chunk(reach(d, halving[::-1], j)) for j in places] for d in n]) for halving in self.halving
        ]
        unit_slot = [np.take_along_axis(np.argsort(c, axis=1), unit_chunk, axis=1) for c in slot_chunk]
        self.tables = np.stack([unit_chunk, *unit_slot, *slot_chunk], axis=1).astype(np.int32)

    def colour(self, device):
        return (device % self.owners).bit_count() & 1

    def partner(self, device, step):
        return device ^ self.masks[step[self.colour(device)]]

    def swap(self, value, step):
        pairs = [(d, self.partner(d, step)) for d in range(self.devices)]
        return lax.ppermute(value, ("grp", "comp"), pairs)


def columns(row, height):
    return jnp.broadcast_to(row, (height, LANES)).T


def copy_kernel(plan, table, *refs):
    sources, copies, sems = refs[:2], refs[2:4], refs[4]
    moves = [pltpu.make_async_copy(s, t, sems.at[i]) for i, (s, t) in enumerate(zip(sources, copies))]
    for move in moves:
        move.start()
    for move in moves:
        move.wait()


def prepare_kernel(plan, table, *refs):
    sources, (stack_ref, staged, features_ref, logits_ref, sems) = refs[:2], refs[2:]
    targets = (features_ref, logits_ref)
    moves = [pltpu.make_async_copy(s, t, sems.at[i]) for i, (s, t) in enumerate(zip(sources, targets))]
    for move in moves:
        move.start()
    for move in moves:
        move.wait()
    logits = logits_ref[...]
    shifted = logits - jnp.max(logits)
    log_weights = shifted - jnp.log(jnp.sum(jnp.exp(shifted)))
    for b in range(logits.shape[0]):
        staged[b * LANES : (b + 1) * LANES, :] = columns(log_weights[b : b + 1, :], LANES)
    width = features_ref.shape[1]
    rows = features_ref[...]
    values = rows.astype(F32)
    squares = values * values
    high = squares.astype(BF16)
    stack_ref[:, :width] = (squares - high.astype(F32)).astype(BF16)
    stack_ref[:, width : 2 * width] = high
    stack_ref[:, 2 * width :] = rows


def build_weights(unit, table, first_units, mean_refs, variance_refs, log_weights, weights, offsets):
    at = 0
    width = mean_refs[0].shape[1]
    for mean_ref, variance_ref, first_unit in zip(mean_refs, variance_refs, first_units):
        for first in range(0, mean_ref.shape[0], unit):
            here = slice(at, at + unit)
            mean = mean_ref[first : first + unit, :]
            variance = variance_ref[first : first + unit, :]
            inverse = 1.0 / variance
            linear = mean * inverse
            constant = jnp.sum(jnp.log(variance) + mean * linear, axis=1, keepdims=True)
            chunk = pl.multiple_of(table[0, first_unit + first // unit] * unit, unit)
            log_weight = log_weights[pl.ds(chunk, unit), :]
            offsets[here, :] = (
                log_weight - 0.5 * constant - 0.5 * width * math.log(2.0 * math.pi)
            ) * LOG2E
            square = inverse * (-0.5 * LOG2E)
            linear = linear * LOG2E
            square_high = square.astype(BF16)
            linear_high = linear.astype(BF16)
            weights[here, :width] = square_high
            weights[here, width : 2 * width] = square_high
            weights[here, 2 * width : 3 * width] = linear_high
            weights[here, 3 * width : 4 * width] = (square - square_high.astype(F32)).astype(BF16)
            weights[here, 4 * width :] = (linear - linear_high.astype(F32)).astype(BF16)
            at += unit


def block_scores(stack, weights, offsets):
    width = stack.shape[1] // 3
    scores = lax.dot_general(
        weights[...],
        jnp.concatenate([stack, stack[:, width:]], axis=1),
        (((1,), (1,)), ((), ())),
        preferred_element_type=F32,
    )
    return scores + jnp.tile(offsets[...], (1, stack.shape[0] // LANES))


def store_moments(plan, table, first_unit, moments, targets):
    unit = plan.unit
    width = moments.shape[1] // 2
    parts = width // LANES
    for u in range(moments.shape[0] // unit):
        for column, target in enumerate(targets):
            slot = table[2 - column, first_unit + u] % (plan.units // 2)
            first = pl.multiple_of(slot * (unit * parts), unit)
            for part in range(parts):
                at = column * width + part * LANES
                target[pl.ds(first + part * unit, unit), :] = moments[
                    u * unit : (u + 1) * unit, at : at + LANES
                ]


def early_kernel(plan, first_units, table, *refs):
    pieces = len(first_units)
    mean_refs, variance_refs = refs[:pieces], refs[pieces : 2 * pieces]
    log_weights, stack_ref, powers_ref, highest_ref, totals_ref, weights, offsets = refs[2 * pieces :]
    count = stack_ref.shape[0]
    block = min(BLOCK, count)
    build_weights(plan.unit, table, first_units, mean_refs, variance_refs, log_weights, weights, offsets)
    for first in range(0, count, block):
        here = slice(first, first + block)
        scores = block_scores(stack_ref[here, :], weights, offsets)
        highest = jnp.max(scores, axis=0, keepdims=True)
        powers = jnp.exp2(scores - highest)
        powers_ref[:, here] = powers
        highest_ref[:, here] = highest
        totals_ref[:, here] = jnp.sum(powers, axis=0, keepdims=True)


def late_kernel(plan, table, *refs):
    mean_ref, variance_ref, log_weights, stack_ref = refs[:4]
    (powers_1, highest_1, totals_1), (powers_2, highest_2, totals_2) = refs[4:7], refs[7:10]
    sent_refs, counts_ref, scores_ref, own_ref = refs[10:12], refs[12], refs[13], refs[14]
    weights, offsets, moments, partial, staged = refs[15:]
    count, width = stack_ref.shape[0], stack_ref.shape[1] // 3
    block = min(2 * BLOCK, count)
    quarter = weights.shape[0]
    firsts = (3 * plan.units // 4,)
    build_weights(plan.unit, table, firsts, (mean_ref,), (variance_ref,), log_weights, weights, offsets)
    for first in range(0, count, block):
        here = slice(first, first + block)
        stack = stack_ref[here, :]
        scores = block_scores(stack, weights, offsets)
        highest = jnp.maximum(
            jnp.maximum(highest_1[:, here], highest_2[:, here]), jnp.max(scores, axis=0, keepdims=True)
        )
        scale_1 = jnp.exp2(highest_1[:, here] - highest)
        scale_2 = jnp.exp2(highest_2[:, here] - highest)
        powers = jnp.exp2(scores - highest)
        totals = (
            totals_1[:, here] * scale_1
            + totals_2[:, here] * scale_2
            + jnp.sum(powers, axis=0, keepdims=True)
        )
        scores_ref[:, here] = (highest + jnp.log2(totals)) * (LN2 / width)
        inverse = 1.0 / totals
        scale_1 = scale_1 * inverse
        scale_2 = scale_2 * inverse
        parts = (
            (powers_1[:quarter, here] * scale_1).astype(BF16),
            (powers_2[:, here] * scale_2).astype(BF16),
            (powers_1[quarter:, here] * scale_1).astype(BF16),
            (powers * inverse).astype(BF16),
        )
        own_ref[:quarter, here] = parts[0]
        own_ref[quarter:, here] = parts[1]
        added = jnp.dot(
            jnp.concatenate(parts[2:], axis=0),
            stack[:, width:],
            preferred_element_type=F32,
        )
        if first == 0:
            moments[...] = added
        else:
            moments[...] += added
        for at, part in enumerate(parts):
            rounded = part.astype(F32)
            counted = rounded[:, :LANES]
            for b in range(1, block // LANES):
                counted = counted + rounded[:, b * LANES : (b + 1) * LANES]
            here = slice(at * quarter, (at + 1) * quarter)
            if first == 0:
                partial[here, :] = counted
            else:
                partial[here, :] += counted

    unit = plan.unit
    for u in range(plan.units):
        chunk = pl.multiple_of(table[0, u] * unit, unit)
        staged[pl.ds(chunk, unit), :] = partial[u * unit : (u + 1) * unit, :]
    half = sent_refs[1].shape[0]
    for b in range(4 * quarter // LANES):
        line = jnp.sum(staged[b * LANES : (b + 1) * LANES, :].T, axis=0, keepdims=True)
        counts_ref[b : b + 1, :] = line
        sent_refs[0][half + b : half + b + 1, :] = line
    store_moments(plan, table, plan.units // 2, moments, sent_refs[::-1])


def own_kernel(plan, table, own_ref, stack_ref, first_ref, second_ref, moments):
    count, width = stack_ref.shape[0], stack_ref.shape[1] // 3
    block = min(BLOCK, count)
    for first in range(0, count, block):
        here = slice(first, first + block)
        added = jnp.dot(own_ref[:, here], stack_ref[here, width:], preferred_element_type=F32)
        if first == 0:
            moments[...] = added
        else:
            moments[...] += added
    store_moments(plan, table, 0, moments, (second_ref, first_ref))


def call(kernel, plan, table, operands, shapes, scratch, flops, vmem_mib, space=pltpu.VMEM):
    vmem = pl.BlockSpec(memory_space=pltpu.VMEM)
    moved = sum(math.prod(o.shape) * o.dtype.itemsize for o in operands)
    return pl.pallas_call(
        functools.partial(kernel, plan),
        in_specs=[pl.BlockSpec(memory_space=pltpu.SMEM)] + [pl.BlockSpec(memory_space=space)] * len(operands),
        out_specs=[vmem] * len(shapes),
        out_shape=[jax.ShapeDtypeStruct(*s) for s in shapes],
        scratch_shapes=[pltpu.VMEM(*s) if isinstance(s, tuple) else s for s in scratch],
        compiler_params=pltpu.CompilerParams(vmem_limit_bytes=vmem_mib * 2**20),
        cost_estimate=pl.CostEstimate(flops=flops, bytes_accessed=2 * moved, transcendentals=0),
    )(table, *operands)


def in_hbm(arrays):
    return [pltpu.with_memory_space_constraint(a, pltpu.HBM) for a in arrays]


def prepare(plan, table, features, logits):
    count, width = features.shape
    comps = math.prod(logits.shape)
    return call(
        prepare_kernel,
        plan,
        table,
        in_hbm([features, logits]),
        [((count, 3 * width), BF16), ((comps, LANES), F32)],
        [((count, width), BF16), (logits.shape, F32), pltpu.SemaphoreType.DMA((2,))],
        8 * count * width,
        16,
        pltpu.HBM,
    )


def early_scores(plan, table, first_units, means, variances, log_weights, stack):
    count, width = stack.shape[0], stack.shape[1] // 3
    comps = sum(m.shape[0] for m in means)
    return call(
        lambda plan, *refs: early_kernel(plan, first_units, *refs),
        plan,
        table,
        [*means, *variances, log_weights, stack],
        [((comps, count), F32), ((1, count), F32), ((1, count), F32)],
        [((comps, 5 * width), BF16), ((comps, LANES), F32)],
        10 * comps * count * width,
        24,
    )


def mixture(plan, table, mean, variance, log_weights, stack, early):
    count, width = stack.shape[0], stack.shape[1] // 3
    half = 2 * mean.shape[0]
    rows = half * (width // LANES)
    *sent, counts, row_scores, own = call(
        late_kernel,
        plan,
        table,
        [mean, variance, log_weights, stack, *early],
        [
            ((rows + COUNT_ROWS, LANES), F32),
            ((rows, LANES), F32),
            ((COUNT_ROWS, LANES), F32),
            ((1, count), F32),
            ((half, count), BF16),
        ],
        [
            ((half // 2, 5 * width), BF16),
            ((half // 2, LANES), F32),
            ((half, 2 * width), F32),
            ((2 * half, LANES), F32),
            ((2 * half, LANES), F32),
        ],
        9 * half * count * width,
        32,
    )
    kept = call(
        own_kernel,
        plan,
        table,
        [own, stack],
        [((rows, LANES), F32)] * 2,
        [((half, 2 * width), F32)],
        4 * half * count * width,
        16,
    )
    return sent, kept, counts, row_scores


def scale_kernel(plan, total_rows, table, counts_ref, log_weights_ref, scale_ref):
    denominator = counts_ref[...] + 1.0
    log_weights_ref[...] = jnp.log(denominator / total_rows)
    inverse = 1.0 / denominator
    for b in range(counts_ref.shape[0]):
        scale_ref[b * LANES : (b + 1) * LANES, :] = columns(inverse[b : b + 1, :], LANES)


def update_kernel(plan, first_slot, table, *refs):
    piece_refs, scale_ref = (refs[:2], refs[2:4]), refs[4]
    means_ref, variances_ref, mean_buffer, variance_buffer, sems = refs[-5:]
    width = mean_buffer.shape[1]
    unit = plan.unit
    parts = width // LANES
    moves = []
    for stream, buffer, target in ((0, mean_buffer, means_ref), (1, variance_buffer, variances_ref)):
        slot = first_slot
        for ref in piece_refs[stream]:
            for first in range(0, ref.shape[0], unit * parts):
                chunk = pl.ds(pl.multiple_of(table[3 + stream, slot] * unit, unit), unit)
                scale = scale_ref[chunk, :]
                for part in range(parts):
                    lanes = slice(part * LANES, (part + 1) * LANES)
                    moment = ref[first + part * unit : first + (part + 1) * unit, :]
                    if stream == 0:
                        buffer[chunk, lanes] = moment * scale
                    else:
                        mean = mean_buffer[chunk, lanes]
                        buffer[chunk, lanes] = (moment + 1.0) * scale - mean * mean + 0.01
                sem = sems.at[stream, slot - first_slot]
                move = pltpu.make_async_copy(buffer.at[chunk, :], target.at[chunk, :], sem)
                move.start()
                moves.append(move)
                slot += 1
    for move in moves:
        move.wait()


def update(plan, table, first_slot, first, second, scale, shape, earlier=()):
    vmem = pl.BlockSpec(memory_space=pltpu.VMEM)
    hbm = pl.BlockSpec(memory_space=pl.ANY)
    operands = [*first, *second, scale]
    return pl.pallas_call(
        functools.partial(update_kernel, plan, first_slot),
        in_specs=[pl.BlockSpec(memory_space=pltpu.SMEM)] + [vmem] * len(operands) + [hbm] * len(earlier),
        out_specs=[hbm] * 2,
        out_shape=[jax.ShapeDtypeStruct(shape, F32)] * 2,
        scratch_shapes=[
            pltpu.VMEM(shape, F32),
            pltpu.VMEM(shape, F32),
            pltpu.SemaphoreType.DMA((2, plan.units // 2)),
        ],
        input_output_aliases={1 + len(operands) + i: i for i in range(len(earlier))},
        compiler_params=pltpu.CompilerParams(vmem_limit_bytes=16 * 2**20),
        cost_estimate=pl.CostEstimate(
            flops=4 * math.prod(shape), bytes_accessed=8 * math.prod(shape), transcendentals=0
        ),
    )(table, *operands, *earlier)


def double(plan, held, step, arrived=None):
    arrived = [plan.swap(h, at) for h, at in zip(held, step)] if arrived is None else arrived
    return [jnp.concatenate(pair, axis=0) for pair in zip(held, arrived)]


def scatter(plan, sent, kept, counts):
    rows = kept[1].shape[0]
    for at, step in enumerate(zip(*plan.halving)):
        if at:
            rows //= 2
            sent = [jnp.concatenate([kept[0][rows:], counts], axis=0), kept[1][rows:]]
            kept = [k[:rows] for k in kept]
        arrived = [plan.swap(s, pair) for s, pair in zip(sent, step)]
        counts = counts + arrived[0][rows:]
        kept = [k + a[:rows] for k, a in zip(kept, arrived)]
    for pair in plan.whole:
        arrived = [plan.swap(jnp.concatenate([kept[0], counts], axis=0), pair), plan.swap(kept[1], pair)]
        counts = counts + arrived[0][rows:]
        kept = [k + a[:rows] for k, a in zip(kept, arrived)]
    return kept, 0.5 * (counts + plan.swap(counts, (0, 0)))


def on_device(plan, features, means, variances, weight_logits):
    comps = weight_logits.shape[0]
    width = means.shape[1]
    me = lax.axis_index(("grp", "comp"))
    table = lax.dynamic_index_in_dim(jnp.asarray(plan.tables), me, 0, keepdims=False)
    logits = weight_logits.reshape(comps // LANES, LANES)

    with jax.named_scope("gather_parameters"):
        arrived = [plan.swap(h, plan.gather[0]) for h in (means, variances)]
        held = call(
            copy_kernel, plan, table, in_hbm([means, variances]), [(means.shape, F32)] * 2,
            [pltpu.SemaphoreType.DMA((2,))], 0, 8, pltpu.HBM,
        )
        held = double(plan, held, None, arrived)
        features, _ = lax.optimization_barrier((features, held[0]))
        stack, log_weights = prepare(plan, table, features, logits)
        for step in plan.gather[1:-1]:
            arrived = [plan.swap(h, step) for h in held]
            arrived[0], stack, log_weights = lax.optimization_barrier((arrived[0], stack, log_weights))
            held = double(plan, held, None, arrived)
        last = [plan.swap(h, plan.gather[-1]) for h in held]
        both = lax.optimization_barrier(held)
        pairs = [(h, plan.swap(b, (0, 0))) for h, b in zip(held, both)]
        firsts = (0, plan.units // 2)
        early = early_scores(plan, table, firsts, *pairs, log_weights, stack)
        last, early = lax.optimization_barrier((last, early))
        mates = [plan.swap(l, (0, 0)) for l in last]
        firsts = (plan.units // 4,)
        early += early_scores(plan, table, firsts, last[:1], last[1:], log_weights, stack)
    sent, kept, counts, row_scores = mixture(plan, table, *mates, log_weights, stack, early)
    with jax.named_scope("scatter_moments"):
        kept, counts = scatter(plan, sent, kept, counts)
    with jax.named_scope("gather_moments"):
        total_rows = float(features.shape[0] * plan.devices + comps)
        log_weights, scale = call(
            lambda plan, *refs: scale_kernel(plan, total_rows, *refs),
            plan,
            table,
            [counts],
            [(counts.shape, F32), ((comps, LANES), F32)],
            [],
            comps,
            8,
        )
        steps = list(zip(*plan.halving))[:0:-1]
        held = kept
        for step in steps[:-1]:
            held = double(plan, held, step)
        last = [plan.swap(h, at) for h, at in zip(held, steps[-1])]
        mates = [plan.swap(h, (0, 0)) for h in held]
        last, scale = lax.optimization_barrier((last, scale))
        own = [[h, l] for h, l in zip(held, last)]
        others = [[m, plan.swap(l, (0, 0))] for m, l in zip(mates, last)]
    fresh = update(plan, table, 0, *own, scale, (comps, width))
    fresh_means, fresh_variances = update(
        plan, table, plan.units // 2, *others, scale, (comps, width), fresh
    )
    return fresh_means, fresh_variances, log_weights.reshape(comps), row_scores.reshape(-1)


def solution(mesh):
    def whole(features, means, variances, weight_logits):
        plan = Plan(mesh.shape["grp"], mesh.shape["comp"], weight_logits.shape[0])
        return jax.shard_map(
            functools.partial(on_device, plan),
            mesh=mesh,
            in_specs=(P(("grp", "comp"), None), P("comp", None), P("comp", None), P()),
            out_specs=(P(), P(), P(), P(("grp", "comp"))),
            check_vma=False,
        )(features, means, variances, weight_logits)

    return whole
```

```python
import functools
import math

import jax
import jax.numpy as jnp
import numpy as np
from jax import lax
from jax.experimental import pallas as pl
from jax.experimental.pallas import tpu as pltpu
from jax.sharding import PartitionSpec as P

F32 = jnp.float32
BF16 = jnp.bfloat16
LANES = 128
COUNT_ROWS = 8
LOG2E = math.log2(math.e)
LN2 = math.log(2.0)
BLOCK = 1024


class Plan:
    def __init__(self, groups, owners, comps):
        self.devices = groups * owners
        self.owners = owners
        owner_bits = owners.bit_length() - 1
        group_bits = groups.bit_length() - 1
        assert owners == 1 << owner_bits and groups == 1 << group_bits
        assert owner_bits >= 4 and group_bits >= 1 and comps % owners == 0
        self.units = owners
        self.unit = comps // owners
        self.masks = [1] + [1 << b | 1 for b in range(1, owner_bits)]
        self.masks += [1 << b for b in range(owner_bits, owner_bits + group_bits)]
        split = [1, owner_bits] + list(range(2, owner_bits - 1))
        rest = [b for b in range(1, owner_bits + group_bits) if b not in split]
        first, second, third, *others = split
        orders = (
            ((third, first, second), (second, third, first)),
            ((first, second, third), (second, third, first)),
        )
        self.halving = [
            [(0, 0)] + list(zip(zero, one)) + [(b, b) for b in others] for zero, one in orders
        ]
        self.whole = [(b, b) for b in rest]
        down = list(range(owner_bits - 1, 0, -1))
        self.gather = list(zip(down, down[:-2] + [down[-1], down[-2]]))

        def reach(device, steps, place):
            for t in reversed(range(len(steps))):
                if place >> t & 1:
                    device = self.partner(device, steps[t])
            return device

        def chunk(device):
            place = sum((device >> b & 1) << i for i, b in enumerate(split)) << 1
            return place | (self.colour(place) ^ self.colour(device))

        n = range(self.devices)
        places = range(self.units)
        unit_chunk = np.array([[reach(d, self.gather + [(0, 0)], p) % owners for p in places] for d in n])
        slot_chunk = [
            np.array([[chunk(reach(d, halving[::-1], j)) for j in places] for d in n]) for halving in self.halving
        ]
        unit_slot = [np.take_along_axis(np.argsort(c, axis=1), unit_chunk, axis=1) for c in slot_chunk]
        self.tables = np.stack([unit_chunk, *unit_slot, *slot_chunk], axis=1).astype(np.int32)

    def colour(self, device):
        return (device % self.owners).bit_count() & 1

    def partner(self, device, step):
        return device ^ self.masks[step[self.colour(device)]]

    def swap(self, value, step):
        pairs = [(d, self.partner(d, step)) for d in range(self.devices)]
        return lax.ppermute(value, ("grp", "comp"), pairs)


def columns(row, height):
    return jnp.broadcast_to(row, (height, LANES)).T


def start_kernel(plan, table, *refs):
    sources, (*copies, staged, logits_ref, sems) = refs[:3], refs[3:]
    targets = (*copies, logits_ref)
    moves = [pltpu.make_async_copy(s, t, sems.at[i]) for i, (s, t) in enumerate(zip(sources, targets))]
    for move in moves:
        move.start()
    for move in moves:
        move.wait()
    logits = logits_ref[...]
    shifted = logits - jnp.max(logits)
    log_weights = shifted - jnp.log(jnp.sum(jnp.exp(shifted)))
    for b in range(logits.shape[0]):
        staged[b * LANES : (b + 1) * LANES, :] = columns(log_weights[b : b + 1, :], LANES)


def stack_kernel(plan, table, source, stack_ref, features_ref, sems):
    count, width = features_ref.shape
    block = count // sems.shape[0]
    moves = []
    for at in range(sems.shape[0]):
        here = pl.ds(at * block, block)
        moves.append(pltpu.make_async_copy(source.at[here], features_ref.at[here], sems.at[at]))
        moves[-1].start()
    for at, move in enumerate(moves):
        move.wait()
        here = slice(at * block, (at + 1) * block)
        rows = features_ref[here, :]
        values = rows.astype(F32)
        squares = values * values
        high = squares.astype(BF16)
        stack_ref[here, :width] = (squares - high.astype(F32)).astype(BF16)
        stack_ref[here, width : 2 * width] = high
        stack_ref[here, 2 * width :] = rows


def build_weights(unit, table, first_units, mean_refs, variance_refs, log_weights, weights, offsets):
    at = 0
    width = mean_refs[0].shape[1]
    for mean_ref, variance_ref, first_unit in zip(mean_refs, variance_refs, first_units):
        for first in range(0, mean_ref.shape[0], unit):
            here = slice(at, at + unit)
            mean = mean_ref[first : first + unit, :]
            variance = variance_ref[first : first + unit, :]
            inverse = 1.0 / variance
            linear = mean * inverse
            constant = jnp.sum(jnp.log(variance) + mean * linear, axis=1, keepdims=True)
            chunk = pl.multiple_of(table[0, first_unit + first // unit] * unit, unit)
            log_weight = log_weights[pl.ds(chunk, unit), :]
            offsets[here, :] = (
                log_weight - 0.5 * constant - 0.5 * width * math.log(2.0 * math.pi)
            ) * LOG2E
            square = inverse * (-0.5 * LOG2E)
            linear = linear * LOG2E
            square_high = square.astype(BF16)
            linear_high = linear.astype(BF16)
            weights[here, :width] = square_high
            weights[here, width : 2 * width] = square_high
            weights[here, 2 * width : 3 * width] = linear_high
            weights[here, 3 * width : 4 * width] = (square - square_high.astype(F32)).astype(BF16)
            weights[here, 4 * width :] = (linear - linear_high.astype(F32)).astype(BF16)
            at += unit


def block_scores(stack, weights, offsets):
    width = stack.shape[1] // 3
    scores = lax.dot_general(
        weights[...],
        jnp.concatenate([stack, stack[:, width:]], axis=1),
        (((1,), (1,)), ((), ())),
        preferred_element_type=F32,
    )
    return scores + jnp.tile(offsets[...], (1, stack.shape[0] // LANES))


def store_moments(plan, table, first_unit, moments, targets):
    unit = plan.unit
    width = moments.shape[1] // 2
    parts = width // LANES
    for u in range(moments.shape[0] // unit):
        for column, target in enumerate(targets):
            slot = table[2 - column, first_unit + u] % (plan.units // 2)
            first = pl.multiple_of(slot * (unit * parts), unit)
            for part in range(parts):
                at = column * width + part * LANES
                target[pl.ds(first + part * unit, unit), :] = moments[
                    u * unit : (u + 1) * unit, at : at + LANES
                ]


def early_kernel(plan, first_units, table, *refs):
    pieces = len(first_units)
    mean_refs, variance_refs = refs[:pieces], refs[pieces : 2 * pieces]
    log_weights, stack_ref, powers_ref, highest_ref, totals_ref, weights, offsets = refs[2 * pieces :]
    count = stack_ref.shape[0]
    block = min(BLOCK, count)
    build_weights(plan.unit, table, first_units, mean_refs, variance_refs, log_weights, weights, offsets)
    for first in range(0, count, block):
        here = slice(first, first + block)
        scores = block_scores(stack_ref[here, :], weights, offsets)
        highest = jnp.max(scores, axis=0, keepdims=True)
        powers = jnp.exp2(scores - highest)
        powers_ref[:, here] = powers
        highest_ref[:, here] = highest
        totals_ref[:, here] = jnp.sum(powers, axis=0, keepdims=True)


def late_kernel(plan, table, *refs):
    mean_ref, variance_ref, log_weights, stack_ref = refs[:4]
    (powers_1, highest_1, totals_1), (powers_2, highest_2, totals_2) = refs[4:7], refs[7:10]
    sent_refs, counts_ref, scores_ref, own_ref = refs[10:12], refs[12], refs[13], refs[14]
    weights, offsets, moments, partial, staged = refs[15:]
    count, width = stack_ref.shape[0], stack_ref.shape[1] // 3
    block = min(2 * BLOCK, count)
    quarter = weights.shape[0]
    firsts = (3 * plan.units // 4,)
    build_weights(plan.unit, table, firsts, (mean_ref,), (variance_ref,), log_weights, weights, offsets)
    for first in range(0, count, block):
        here = slice(first, first + block)
        stack = stack_ref[here, :]
        scores = block_scores(stack, weights, offsets)
        highest = jnp.maximum(
            jnp.maximum(highest_1[:, here], highest_2[:, here]), jnp.max(scores, axis=0, keepdims=True)
        )
        scale_1 = jnp.exp2(highest_1[:, here] - highest)
        scale_2 = jnp.exp2(highest_2[:, here] - highest)
        powers = jnp.exp2(scores - highest)
        totals = (
            totals_1[:, here] * scale_1
            + totals_2[:, here] * scale_2
            + jnp.sum(powers, axis=0, keepdims=True)
        )
        scores_ref[:, here] = (highest + jnp.log2(totals)) * (LN2 / width)
        inverse = 1.0 / totals
        scale_1 = scale_1 * inverse
        scale_2 = scale_2 * inverse
        parts = (
            (powers_1[:quarter, here] * scale_1).astype(BF16),
            (powers_2[:, here] * scale_2).astype(BF16),
            (powers_1[quarter:, here] * scale_1).astype(BF16),
            (powers * inverse).astype(BF16),
        )
        own_ref[:quarter, here] = parts[0]
        own_ref[quarter:, here] = parts[1]
        added = jnp.dot(
            jnp.concatenate(parts[2:], axis=0),
            stack[:, width:],
            preferred_element_type=F32,
        )
        if first == 0:
            moments[...] = added
        else:
            moments[...] += added
        for at, part in enumerate(parts):
            rounded = part.astype(F32)
            counted = rounded[:, :LANES]
            for b in range(1, block // LANES):
                counted = counted + rounded[:, b * LANES : (b + 1) * LANES]
            here = slice(at * quarter, (at + 1) * quarter)
            if first == 0:
                partial[here, :] = counted
            else:
                partial[here, :] += counted

    unit = plan.unit
    for u in range(plan.units):
        chunk = pl.multiple_of(table[0, u] * unit, unit)
        staged[pl.ds(chunk, unit), :] = partial[u * unit : (u + 1) * unit, :]
    half = sent_refs[1].shape[0]
    for b in range(4 * quarter // LANES):
        line = jnp.sum(staged[b * LANES : (b + 1) * LANES, :].T, axis=0, keepdims=True)
        counts_ref[b : b + 1, :] = line
        sent_refs[0][half + b : half + b + 1, :] = line
    store_moments(plan, table, plan.units // 2, moments, sent_refs[::-1])


def own_kernel(plan, table, own_ref, stack_ref, first_ref, second_ref, moments):
    count, width = stack_ref.shape[0], stack_ref.shape[1] // 3
    block = min(BLOCK, count)
    for first in range(0, count, block):
        here = slice(first, first + block)
        added = jnp.dot(own_ref[:, here], stack_ref[here, width:], preferred_element_type=F32)
        if first == 0:
            moments[...] = added
        else:
            moments[...] += added
    store_moments(plan, table, 0, moments, (second_ref, first_ref))


def call(kernel, plan, table, operands, shapes, scratch, flops, vmem_mib, space=pltpu.VMEM):
    vmem = pl.BlockSpec(memory_space=pltpu.VMEM)
    moved = sum(math.prod(o.shape) * o.dtype.itemsize for o in operands)
    return pl.pallas_call(
        functools.partial(kernel, plan),
        in_specs=[pl.BlockSpec(memory_space=pltpu.SMEM)] + [pl.BlockSpec(memory_space=space)] * len(operands),
        out_specs=[vmem] * len(shapes),
        out_shape=[jax.ShapeDtypeStruct(*s) for s in shapes],
        scratch_shapes=[pltpu.VMEM(*s) if isinstance(s, tuple) else s for s in scratch],
        compiler_params=pltpu.CompilerParams(vmem_limit_bytes=vmem_mib * 2**20),
        cost_estimate=pl.CostEstimate(flops=flops, bytes_accessed=2 * moved, transcendentals=0),
    )(table, *operands)


def in_hbm(arrays):
    return [pltpu.with_memory_space_constraint(a, pltpu.HBM) for a in arrays]


def own_copies(plan, table, means, variances, logits):
    return call(
        start_kernel,
        plan,
        table,
        in_hbm([means, variances, logits]),
        [(means.shape, F32)] * 2 + [((math.prod(logits.shape), LANES), F32)],
        [(logits.shape, F32), pltpu.SemaphoreType.DMA((3,))],
        0,
        8,
        pltpu.HBM,
    )


def feature_stack(plan, table, features):
    count, width = features.shape
    return call(
        stack_kernel,
        plan,
        table,
        in_hbm([features]),
        [((count, 3 * width), BF16)],
        [((count, width), BF16), pltpu.SemaphoreType.DMA((4,))],
        8 * count * width,
        16,
        pltpu.HBM,
    )[0]


def early_scores(plan, table, first_units, means, variances, log_weights, stack):
    count, width = stack.shape[0], stack.shape[1] // 3
    comps = sum(m.shape[0] for m in means)
    return call(
        lambda plan, *refs: early_kernel(plan, first_units, *refs),
        plan,
        table,
        [*means, *variances, log_weights, stack],
        [((comps, count), F32), ((1, count), F32), ((1, count), F32)],
        [((comps, 5 * width), BF16), ((comps, LANES), F32)],
        10 * comps * count * width,
        24,
    )


def mixture(plan, table, mean, variance, log_weights, stack, early):
    count, width = stack.shape[0], stack.shape[1] // 3
    half = 2 * mean.shape[0]
    rows = half * (width // LANES)
    *sent, counts, row_scores, own = call(
        late_kernel,
        plan,
        table,
        [mean, variance, log_weights, stack, *early],
        [
            ((rows + COUNT_ROWS, LANES), F32),
            ((rows, LANES), F32),
            ((COUNT_ROWS, LANES), F32),
            ((1, count), F32),
            ((half, count), BF16),
        ],
        [
            ((half // 2, 5 * width), BF16),
            ((half // 2, LANES), F32),
            ((half, 2 * width), F32),
            ((2 * half, LANES), F32),
            ((2 * half, LANES), F32),
        ],
        9 * half * count * width,
        32,
    )
    kept = call(
        own_kernel,
        plan,
        table,
        [own, stack],
        [((rows, LANES), F32)] * 2,
        [((half, 2 * width), F32)],
        4 * half * count * width,
        16,
    )
    return sent, kept, counts, row_scores


def scale_kernel(plan, total_rows, table, counts_ref, log_weights_ref, scale_ref):
    denominator = counts_ref[...] + 1.0
    log_weights_ref[...] = jnp.log(denominator / total_rows)
    inverse = 1.0 / denominator
    for b in range(counts_ref.shape[0]):
        scale_ref[b * LANES : (b + 1) * LANES, :] = columns(inverse[b : b + 1, :], LANES)


def update_kernel(plan, first_slot, table, *refs):
    piece_refs, scale_ref = (refs[:2], refs[2:4]), refs[4]
    means_ref, variances_ref, mean_buffer, variance_buffer, sems = refs[-5:]
    width = mean_buffer.shape[1]
    unit = plan.unit
    parts = width // LANES
    moves = []
    for stream, buffer, target in ((0, mean_buffer, means_ref), (1, variance_buffer, variances_ref)):
        slot = first_slot
        for ref in piece_refs[stream]:
            for first in range(0, ref.shape[0], unit * parts):
                chunk = pl.ds(pl.multiple_of(table[3 + stream, slot] * unit, unit), unit)
                scale = scale_ref[chunk, :]
                for part in range(parts):
                    lanes = slice(part * LANES, (part + 1) * LANES)
                    moment = ref[first + part * unit : first + (part + 1) * unit, :]
                    if stream == 0:
                        buffer[chunk, lanes] = moment * scale
                    else:
                        mean = mean_buffer[chunk, lanes]
                        buffer[chunk, lanes] = (moment + 1.0) * scale - mean * mean + 0.01
                sem = sems.at[stream, slot - first_slot]
                move = pltpu.make_async_copy(buffer.at[chunk, :], target.at[chunk, :], sem)
                move.start()
                moves.append(move)
                slot += 1
    for move in moves:
        move.wait()


def update(plan, table, first_slot, first, second, scale, shape, earlier=()):
    vmem = pl.BlockSpec(memory_space=pltpu.VMEM)
    hbm = pl.BlockSpec(memory_space=pl.ANY)
    operands = [*first, *second, scale]
    return pl.pallas_call(
        functools.partial(update_kernel, plan, first_slot),
        in_specs=[pl.BlockSpec(memory_space=pltpu.SMEM)] + [vmem] * len(operands) + [hbm] * len(earlier),
        out_specs=[hbm] * 2,
        out_shape=[jax.ShapeDtypeStruct(shape, F32)] * 2,
        scratch_shapes=[
            pltpu.VMEM(shape, F32),
            pltpu.VMEM(shape, F32),
            pltpu.SemaphoreType.DMA((2, plan.units // 2)),
        ],
        input_output_aliases={1 + len(operands) + i: i for i in range(len(earlier))},
        compiler_params=pltpu.CompilerParams(vmem_limit_bytes=16 * 2**20),
        cost_estimate=pl.CostEstimate(
            flops=4 * math.prod(shape), bytes_accessed=8 * math.prod(shape), transcendentals=0
        ),
    )(table, *operands, *earlier)


def double(plan, held, step, arrived=None):
    arrived = [plan.swap(h, at) for h, at in zip(held, step)] if arrived is None else arrived
    return [jnp.concatenate(pair, axis=0) for pair in zip(held, arrived)]


def scatter(plan, sent, kept, counts):
    rows = kept[1].shape[0]
    for at, step in enumerate(zip(*plan.halving)):
        if at:
            rows //= 2
            sent = [jnp.concatenate([kept[0][rows:], counts], axis=0), kept[1][rows:]]
            kept = [k[:rows] for k in kept]
        arrived = [plan.swap(s, pair) for s, pair in zip(sent, step)]
        counts = counts + arrived[0][rows:]
        kept = [k + a[:rows] for k, a in zip(kept, arrived)]
    for pair in plan.whole:
        arrived = [plan.swap(jnp.concatenate([kept[0], counts], axis=0), pair), plan.swap(kept[1], pair)]
        counts = counts + arrived[0][rows:]
        first = kept[0] + arrived[0][:rows]
        second, _ = lax.optimization_barrier((arrived[1], first))
        kept = [first, kept[1] + second]
    return kept, 0.5 * (counts + plan.swap(counts, (0, 0)))


def on_device(plan, features, means, variances, weight_logits):
    comps = weight_logits.shape[0]
    width = means.shape[1]
    me = lax.axis_index(("grp", "comp"))
    table = lax.dynamic_index_in_dim(jnp.asarray(plan.tables), me, 0, keepdims=False)
    logits = weight_logits.reshape(comps // LANES, LANES)

    with jax.named_scope("gather_parameters"):
        arrived = [plan.swap(h, plan.gather[0]) for h in (means, variances)]
        *held, log_weights = own_copies(plan, table, means, variances, logits)
        stack = feature_stack(plan, table, features)
        arrived[1], stack = lax.optimization_barrier((arrived[1], stack))
        held = double(plan, held, None, arrived)
        for step in plan.gather[1:-1]:
            held = double(plan, held, (step, step))
        last = [plan.swap(h, plan.gather[-1]) for h in held]
        both = lax.optimization_barrier(held)
        pairs = [(h, plan.swap(b, (0, 0))) for h, b in zip(held, both)]
        firsts = (0, plan.units // 2)
        early = early_scores(plan, table, firsts, *pairs, log_weights, stack)
        last, early = lax.optimization_barrier((last, early))
        mates = [plan.swap(l, (0, 0)) for l in last]
        firsts = (plan.units // 4,)
        early += early_scores(plan, table, firsts, last[:1], last[1:], log_weights, stack)
    sent, kept, counts, row_scores = mixture(plan, table, *mates, log_weights, stack, early)
    with jax.named_scope("scatter_moments"):
        kept, counts = scatter(plan, sent, kept, counts)
    with jax.named_scope("gather_moments"):
        total_rows = float(features.shape[0] * plan.devices + comps)
        log_weights, scale = call(
            lambda plan, *refs: scale_kernel(plan, total_rows, *refs),
            plan,
            table,
            [counts],
            [(counts.shape, F32), ((comps, LANES), F32)],
            [],
            comps,
            8,
        )
        steps = list(zip(*plan.halving))[:0:-1]
        held = kept
        for step in steps[:-1]:
            held = double(plan, held, step)
        last = [plan.swap(h, at) for h, at in zip(held, steps[-1])]
        mates = [plan.swap(h, (0, 0)) for h in held]
        last, scale = lax.optimization_barrier((last, scale))
        own = [[h, l] for h, l in zip(held, last)]
        others = [[m, plan.swap(l, (0, 0))] for m, l in zip(mates, last)]
    fresh = update(plan, table, 0, *own, scale, (comps, width))
    fresh_means, fresh_variances = update(
        plan, table, plan.units // 2, *others, scale, (comps, width), fresh
    )
    return fresh_means, fresh_variances, log_weights.reshape(comps), row_scores.reshape(-1)


def solution(mesh):
    def whole(features, means, variances, weight_logits):
        plan = Plan(mesh.shape["grp"], mesh.shape["comp"], weight_logits.shape[0])
        return jax.shard_map(
            functools.partial(on_device, plan),
            mesh=mesh,
            in_specs=(P(("grp", "comp"), None), P("comp", None), P("comp", None), P()),
            out_specs=(P(), P(), P(), P(("grp", "comp"))),
            check_vma=False,
        )(features, means, variances, weight_logits)

    return whole
```

```python
import functools
import math

import jax
import jax.numpy as jnp
import numpy as np
from jax import lax
from jax.experimental import pallas as pl
from jax.experimental.pallas import tpu as pltpu
from jax.sharding import PartitionSpec as P

F32 = jnp.float32
BF16 = jnp.bfloat16
LANES = 128
COUNT_ROWS = 8
LOG2E = math.log2(math.e)
LN2 = math.log(2.0)
BLOCK = 1024


class Plan:
    def __init__(self, groups, owners, comps):
        self.devices = groups * owners
        self.owners = owners
        owner_bits = owners.bit_length() - 1
        group_bits = groups.bit_length() - 1
        assert owners == 1 << owner_bits and groups == 1 << group_bits
        assert owner_bits >= 4 and group_bits >= 1 and comps % owners == 0
        self.units = owners
        self.unit = comps // owners
        self.masks = [1] + [1 << b | 1 for b in range(1, owner_bits)]
        self.masks += [1 << b for b in range(owner_bits, owner_bits + group_bits)]
        split = [1, owner_bits] + list(range(2, owner_bits - 1))
        rest = [b for b in range(1, owner_bits + group_bits) if b not in split]
        first, second, third, *others = split
        orders = (
            ((third, first, second), (second, third, first)),
            ((first, second, third), (second, third, first)),
        )
        self.halving = [
            [(0, 0)] + list(zip(zero, one)) + [(b, b) for b in others] for zero, one in orders
        ]
        self.whole = [(b, b) for b in rest]
        down = list(range(owner_bits - 1, 0, -1))
        self.gather = list(zip(down, down[:-2] + [down[-1], down[-2]]))

        def reach(device, steps, place):
            for t in reversed(range(len(steps))):
                if place >> t & 1:
                    device = self.partner(device, steps[t])
            return device

        def chunk(device):
            place = sum((device >> b & 1) << i for i, b in enumerate(split)) << 1
            return place | (self.colour(place) ^ self.colour(device))

        n = range(self.devices)
        places = range(self.units)
        unit_chunk = np.array([[reach(d, self.gather + [(0, 0)], p) % owners for p in places] for d in n])
        slot_chunk = [
            np.array([[chunk(reach(d, halving[::-1], j)) for j in places] for d in n]) for halving in self.halving
        ]
        unit_slot = [np.take_along_axis(np.argsort(c, axis=1), unit_chunk, axis=1) for c in slot_chunk]
        self.tables = np.stack([unit_chunk, *unit_slot, *slot_chunk], axis=1).astype(np.int32)

    def colour(self, device):
        return (device % self.owners).bit_count() & 1

    def partner(self, device, step):
        return device ^ self.masks[step[self.colour(device)]]

    def swap(self, value, step):
        pairs = [(d, self.partner(d, step)) for d in range(self.devices)]
        return lax.ppermute(value, ("grp", "comp"), pairs)


def columns(row, height):
    return jnp.broadcast_to(row, (height, LANES)).T


def start_kernel(plan, table, *refs):
    sources, (*copies, staged, logits_ref, sems) = refs[:3], refs[3:]
    targets = (*copies, logits_ref)
    moves = [pltpu.make_async_copy(s, t, sems.at[i]) for i, (s, t) in enumerate(zip(sources, targets))]
    for move in moves:
        move.start()
    for move in moves:
        move.wait()
    logits = logits_ref[...]
    shifted = logits - jnp.max(logits)
    log_weights = shifted - jnp.log(jnp.sum(jnp.exp(shifted)))
    for b in range(logits.shape[0]):
        staged[b * LANES : (b + 1) * LANES, :] = columns(log_weights[b : b + 1, :], LANES)


def stack_kernel(plan, table, source, stack_ref, features_ref, sems):
    count, width = features_ref.shape
    block = count // sems.shape[0]
    moves = []
    for at in range(sems.shape[0]):
        here = pl.ds(at * block, block)
        moves.append(pltpu.make_async_copy(source.at[here], features_ref.at[here], sems.at[at]))
        moves[-1].start()
    for at, move in enumerate(moves):
        move.wait()
        here = slice(at * block, (at + 1) * block)
        rows = features_ref[here, :]
        values = rows.astype(F32)
        squares = values * values
        high = squares.astype(BF16)
        stack_ref[here, :width] = (squares - high.astype(F32)).astype(BF16)
        stack_ref[here, width : 2 * width] = high
        stack_ref[here, 2 * width :] = rows


def build_weights(unit, table, first_units, mean_refs, variance_refs, log_weights, weights, offsets):
    at = 0
    width = mean_refs[0].shape[1]
    for mean_ref, variance_ref, first_unit in zip(mean_refs, variance_refs, first_units):
        for first in range(0, mean_ref.shape[0], unit):
            here = slice(at, at + unit)
            mean = mean_ref[first : first + unit, :]
            variance = variance_ref[first : first + unit, :]
            inverse = 1.0 / variance
            linear = mean * inverse
            constant = jnp.sum(jnp.log(variance) + mean * linear, axis=1, keepdims=True)
            chunk = pl.multiple_of(table[0, first_unit + first // unit] * unit, unit)
            log_weight = log_weights[pl.ds(chunk, unit), :]
            offsets[here, :] = (
                log_weight - 0.5 * constant - 0.5 * width * math.log(2.0 * math.pi)
            ) * LOG2E
            square = inverse * (-0.5 * LOG2E)
            linear = linear * LOG2E
            square_high = square.astype(BF16)
            linear_high = linear.astype(BF16)
            weights[here, :width] = square_high
            weights[here, width : 2 * width] = square_high
            weights[here, 2 * width : 3 * width] = linear_high
            weights[here, 3 * width : 4 * width] = (square - square_high.astype(F32)).astype(BF16)
            weights[here, 4 * width :] = (linear - linear_high.astype(F32)).astype(BF16)
            at += unit


def block_scores(stack, weights, offsets):
    width = stack.shape[1] // 3
    scores = lax.dot_general(
        weights[...],
        jnp.concatenate([stack, stack[:, width:]], axis=1),
        (((1,), (1,)), ((), ())),
        preferred_element_type=F32,
    )
    return scores + jnp.tile(offsets[...], (1, stack.shape[0] // LANES))


def store_moments(plan, table, first_unit, moments, targets):
    unit = plan.unit
    width = moments.shape[1] // 2
    parts = width // LANES
    for u in range(moments.shape[0] // unit):
        for column, target in enumerate(targets):
            slot = table[2 - column, first_unit + u] % (plan.units // 2)
            first = pl.multiple_of(slot * (unit * parts), unit)
            for part in range(parts):
                at = column * width + part * LANES
                target[pl.ds(first + part * unit, unit), :] = moments[
                    u * unit : (u + 1) * unit, at : at + LANES
                ]


def early_kernel(plan, first_units, table, *refs):
    pieces = len(first_units)
    mean_refs, variance_refs = refs[:pieces], refs[pieces : 2 * pieces]
    log_weights, stack_ref, powers_ref, highest_ref, totals_ref, weights, offsets = refs[2 * pieces :]
    count = stack_ref.shape[0]
    block = min(BLOCK, count)
    build_weights(plan.unit, table, first_units, mean_refs, variance_refs, log_weights, weights, offsets)
    for first in range(0, count, block):
        here = slice(first, first + block)
        scores = block_scores(stack_ref[here, :], weights, offsets)
        highest = jnp.max(scores, axis=0, keepdims=True)
        powers = jnp.exp2(scores - highest)
        powers_ref[:, here] = powers
        highest_ref[:, here] = highest
        totals_ref[:, here] = jnp.sum(powers, axis=0, keepdims=True)


def late_kernel(plan, table, *refs):
    mean_ref, variance_ref, log_weights, stack_ref = refs[:4]
    (powers_1, highest_1, totals_1), (powers_2, highest_2, totals_2) = refs[4:7], refs[7:10]
    sent_refs, counts_ref, scores_ref, own_ref = refs[10:12], refs[12], refs[13], refs[14]
    weights, offsets, moments, partial, staged = refs[15:]
    count, width = stack_ref.shape[0], stack_ref.shape[1] // 3
    block = min(2 * BLOCK, count)
    quarter = weights.shape[0]
    firsts = (3 * plan.units // 4,)
    build_weights(plan.unit, table, firsts, (mean_ref,), (variance_ref,), log_weights, weights, offsets)
    for first in range(0, count, block):
        here = slice(first, first + block)
        stack = stack_ref[here, :]
        scores = block_scores(stack, weights, offsets)
        highest = jnp.maximum(
            jnp.maximum(highest_1[:, here], highest_2[:, here]), jnp.max(scores, axis=0, keepdims=True)
        )
        scale_1 = jnp.exp2(highest_1[:, here] - highest)
        scale_2 = jnp.exp2(highest_2[:, here] - highest)
        powers = jnp.exp2(scores - highest)
        totals = (
            totals_1[:, here] * scale_1
            + totals_2[:, here] * scale_2
            + jnp.sum(powers, axis=0, keepdims=True)
        )
        scores_ref[:, here] = (highest + jnp.log2(totals)) * (LN2 / width)
        inverse = 1.0 / totals
        scale_1 = scale_1 * inverse
        scale_2 = scale_2 * inverse
        parts = (
            (powers_1[:quarter, here] * scale_1).astype(BF16),
            (powers_2[:, here] * scale_2).astype(BF16),
            (powers_1[quarter:, here] * scale_1).astype(BF16),
            (powers * inverse).astype(BF16),
        )
        own_ref[:quarter, here] = parts[0]
        own_ref[quarter:, here] = parts[1]
        added = jnp.dot(
            jnp.concatenate(parts[2:], axis=0),
            stack[:, width:],
            preferred_element_type=F32,
        )
        if first == 0:
            moments[...] = added
        else:
            moments[...] += added
        for at, part in enumerate(parts):
            rounded = part.astype(F32)
            counted = rounded[:, :LANES]
            for b in range(1, block // LANES):
                counted = counted + rounded[:, b * LANES : (b + 1) * LANES]
            here = slice(at * quarter, (at + 1) * quarter)
            if first == 0:
                partial[here, :] = counted
            else:
                partial[here, :] += counted

    unit = plan.unit
    for u in range(plan.units):
        chunk = pl.multiple_of(table[0, u] * unit, unit)
        staged[pl.ds(chunk, unit), :] = partial[u * unit : (u + 1) * unit, :]
    half = sent_refs[1].shape[0]
    for b in range(4 * quarter // LANES):
        line = jnp.sum(staged[b * LANES : (b + 1) * LANES, :].T, axis=0, keepdims=True)
        counts_ref[b : b + 1, :] = line
        sent_refs[0][half + b : half + b + 1, :] = line
    store_moments(plan, table, plan.units // 2, moments, sent_refs[::-1])


def own_kernel(plan, stream, table, own_ref, stack_ref, moments_ref):
    width = stack_ref.shape[1] // 3
    unit = plan.unit
    parts = width // LANES
    inputs = stack_ref[:, (2 - stream) * width : (3 - stream) * width]
    moments = jnp.dot(own_ref[...], inputs, preferred_element_type=F32)
    for u in range(plan.units // 2):
        slot = table[1 + stream, u] % (plan.units // 2)
        first = pl.multiple_of(slot * (unit * parts), unit)
        for part in range(parts):
            moments_ref[pl.ds(first + part * unit, unit), :] = moments[
                u * unit : (u + 1) * unit, part * LANES : (part + 1) * LANES
            ]


def call(kernel, plan, table, operands, shapes, scratch, flops, vmem_mib, space=pltpu.VMEM):
    vmem = pl.BlockSpec(memory_space=pltpu.VMEM)
    moved = sum(math.prod(o.shape) * o.dtype.itemsize for o in operands)
    return pl.pallas_call(
        functools.partial(kernel, plan),
        in_specs=[pl.BlockSpec(memory_space=pltpu.SMEM)] + [pl.BlockSpec(memory_space=space)] * len(operands),
        out_specs=[vmem] * len(shapes),
        out_shape=[jax.ShapeDtypeStruct(*s) for s in shapes],
        scratch_shapes=[pltpu.VMEM(*s) if isinstance(s, tuple) else s for s in scratch],
        compiler_params=pltpu.CompilerParams(vmem_limit_bytes=vmem_mib * 2**20),
        cost_estimate=pl.CostEstimate(flops=flops, bytes_accessed=2 * moved, transcendentals=0),
    )(table, *operands)


def in_hbm(arrays):
    return [pltpu.with_memory_space_constraint(a, pltpu.HBM) for a in arrays]


def own_copies(plan, table, means, variances, logits):
    return call(
        start_kernel,
        plan,
        table,
        in_hbm([means, variances, logits]),
        [(means.shape, F32)] * 2 + [((math.prod(logits.shape), LANES), F32)],
        [(logits.shape, F32), pltpu.SemaphoreType.DMA((3,))],
        0,
        8,
        pltpu.HBM,
    )


def feature_stack(plan, table, features):
    count, width = features.shape
    return call(
        stack_kernel,
        plan,
        table,
        in_hbm([features]),
        [((count, 3 * width), BF16)],
        [((count, width), BF16), pltpu.SemaphoreType.DMA((4,))],
        8 * count * width,
        16,
        pltpu.HBM,
    )[0]


def early_scores(plan, table, first_units, means, variances, log_weights, stack):
    count, width = stack.shape[0], stack.shape[1] // 3
    comps = sum(m.shape[0] for m in means)
    return call(
        lambda plan, *refs: early_kernel(plan, first_units, *refs),
        plan,
        table,
        [*means, *variances, log_weights, stack],
        [((comps, count), F32), ((1, count), F32), ((1, count), F32)],
        [((comps, 5 * width), BF16), ((comps, LANES), F32)],
        10 * comps * count * width,
        24,
    )


def mixture(plan, table, mean, variance, log_weights, stack, early):
    count, width = stack.shape[0], stack.shape[1] // 3
    half = 2 * mean.shape[0]
    rows = half * (width // LANES)
    *sent, counts, row_scores, own = call(
        late_kernel,
        plan,
        table,
        [mean, variance, log_weights, stack, *early],
        [
            ((rows + COUNT_ROWS, LANES), F32),
            ((rows, LANES), F32),
            ((COUNT_ROWS, LANES), F32),
            ((1, count), F32),
            ((half, count), BF16),
        ],
        [
            ((half // 2, 5 * width), BF16),
            ((half // 2, LANES), F32),
            ((half, 2 * width), F32),
            ((2 * half, LANES), F32),
            ((2 * half, LANES), F32),
        ],
        9 * half * count * width,
        32,
    )
    kept = [
        call(
            lambda plan, *refs, stream=stream: own_kernel(plan, stream, *refs),
            plan,
            table,
            [own, stack],
            [((rows, LANES), F32)],
            [],
            2 * half * count * width,
            16,
        )[0]
        for stream in (0, 1)
    ]
    return sent, kept, counts, row_scores


def scale_kernel(plan, total_rows, table, counts_ref, log_weights_ref, scale_ref):
    denominator = counts_ref[...] + 1.0
    log_weights_ref[...] = jnp.log(denominator / total_rows)
    inverse = 1.0 / denominator
    for b in range(counts_ref.shape[0]):
        scale_ref[b * LANES : (b + 1) * LANES, :] = columns(inverse[b : b + 1, :], LANES)


def update_kernel(plan, first_slot, table, *refs):
    piece_refs, scale_ref = (refs[:2], refs[2:4]), refs[4]
    means_ref, variances_ref, mean_buffer, variance_buffer, sems = refs[-5:]
    width = mean_buffer.shape[1]
    unit = plan.unit
    parts = width // LANES
    moves = []
    for stream, buffer, target in ((0, mean_buffer, means_ref), (1, variance_buffer, variances_ref)):
        slot = first_slot
        for ref in piece_refs[stream]:
            for first in range(0, ref.shape[0], unit * parts):
                chunk = pl.ds(pl.multiple_of(table[3 + stream, slot] * unit, unit), unit)
                scale = scale_ref[chunk, :]
                for part in range(parts):
                    lanes = slice(part * LANES, (part + 1) * LANES)
                    moment = ref[first + part * unit : first + (part + 1) * unit, :]
                    if stream == 0:
                        buffer[chunk, lanes] = moment * scale
                    else:
                        mean = mean_buffer[chunk, lanes]
                        buffer[chunk, lanes] = (moment + 1.0) * scale - mean * mean + 0.01
                sem = sems.at[stream, slot - first_slot]
                move = pltpu.make_async_copy(buffer.at[chunk, :], target.at[chunk, :], sem)
                move.start()
                moves.append(move)
                slot += 1
    for move in moves:
        move.wait()


def update(plan, table, first_slot, first, second, scale, shape, earlier=()):
    vmem = pl.BlockSpec(memory_space=pltpu.VMEM)
    hbm = pl.BlockSpec(memory_space=pl.ANY)
    operands = [*first, *second, scale]
    return pl.pallas_call(
        functools.partial(update_kernel, plan, first_slot),
        in_specs=[pl.BlockSpec(memory_space=pltpu.SMEM)] + [vmem] * len(operands) + [hbm] * len(earlier),
        out_specs=[hbm] * 2,
        out_shape=[jax.ShapeDtypeStruct(shape, F32)] * 2,
        scratch_shapes=[
            pltpu.VMEM(shape, F32),
            pltpu.VMEM(shape, F32),
            pltpu.SemaphoreType.DMA((2, plan.units // 2)),
        ],
        input_output_aliases={1 + len(operands) + i: i for i in range(len(earlier))},
        compiler_params=pltpu.CompilerParams(vmem_limit_bytes=16 * 2**20),
        cost_estimate=pl.CostEstimate(
            flops=4 * math.prod(shape), bytes_accessed=8 * math.prod(shape), transcendentals=0
        ),
    )(table, *operands, *earlier)


def double(plan, held, step, arrived=None):
    arrived = [plan.swap(h, at) for h, at in zip(held, step)] if arrived is None else arrived
    return [jnp.concatenate(pair, axis=0) for pair in zip(held, arrived)]


def scatter(plan, sent, kept, counts):
    rows = kept[1].shape[0]
    for at, step in enumerate(zip(*plan.halving)):
        if at:
            rows //= 2
            sent = [jnp.concatenate([kept[0][rows:], counts], axis=0), kept[1][rows:]]
            kept = [k[:rows] for k in kept]
        arrived = [plan.swap(s, pair) for s, pair in zip(sent, step)]
        counts = counts + arrived[0][rows:]
        kept = [k + a[:rows] for k, a in zip(kept, arrived)]
    for pair in plan.whole:
        arrived = [plan.swap(jnp.concatenate([kept[0], counts], axis=0), pair), plan.swap(kept[1], pair)]
        counts = counts + arrived[0][rows:]
        first = kept[0] + arrived[0][:rows]
        second, _ = lax.optimization_barrier((arrived[1], first))
        kept = [first, kept[1] + second]
    return kept, 0.5 * (counts + plan.swap(counts, (0, 0)))


def on_device(plan, features, means, variances, weight_logits):
    comps = weight_logits.shape[0]
    width = means.shape[1]
    me = lax.axis_index(("grp", "comp"))
    table = lax.dynamic_index_in_dim(jnp.asarray(plan.tables), me, 0, keepdims=False)
    logits = weight_logits.reshape(comps // LANES, LANES)

    with jax.named_scope("gather_parameters"):
        arrived = [plan.swap(h, plan.gather[0]) for h in (means, variances)]
        *held, log_weights = own_copies(plan, table, means, variances, logits)
        stack = feature_stack(plan, table, features)
        arrived[1], stack = lax.optimization_barrier((arrived[1], stack))
        held = double(plan, held, None, arrived)
        for step in plan.gather[1:-1]:
            held = double(plan, held, (step, step))
        last = [plan.swap(h, plan.gather[-1]) for h in held]
        both = lax.optimization_barrier(held)
        pairs = [(h, plan.swap(b, (0, 0))) for h, b in zip(held, both)]
        firsts = (0, plan.units // 2)
        early = early_scores(plan, table, firsts, *pairs, log_weights, stack)
        last, early = lax.optimization_barrier((last, early))
        mates = [plan.swap(l, (0, 0)) for l in last]
        firsts = (plan.units // 4,)
        early += early_scores(plan, table, firsts, last[:1], last[1:], log_weights, stack)
    sent, kept, counts, row_scores = mixture(plan, table, *mates, log_weights, stack, early)
    with jax.named_scope("scatter_moments"):
        kept, counts = scatter(plan, sent, kept, counts)
    with jax.named_scope("gather_moments"):
        total_rows = float(features.shape[0] * plan.devices + comps)
        log_weights, scale = call(
            lambda plan, *refs: scale_kernel(plan, total_rows, *refs),
            plan,
            table,
            [counts],
            [(counts.shape, F32), ((comps, LANES), F32)],
            [],
            comps,
            8,
        )
        steps = list(zip(*plan.halving))[:0:-1]
        held = kept
        for step in steps[:-1]:
            held = double(plan, held, step)
        last = [plan.swap(h, at) for h, at in zip(held, steps[-1])]
        mates = [plan.swap(h, (0, 0)) for h in held]
        last, scale = lax.optimization_barrier((last, scale))
        own = [[h, l] for h, l in zip(held, last)]
        others = [[m, plan.swap(l, (0, 0))] for m, l in zip(mates, last)]
    fresh = update(plan, table, 0, *own, scale, (comps, width))
    fresh_means, fresh_variances = update(
        plan, table, plan.units // 2, *others, scale, (comps, width), fresh
    )
    return fresh_means, fresh_variances, log_weights.reshape(comps), row_scores.reshape(-1)


def solution(mesh):
    def whole(features, means, variances, weight_logits):
        plan = Plan(mesh.shape["grp"], mesh.shape["comp"], weight_logits.shape[0])
        return jax.shard_map(
            functools.partial(on_device, plan),
            mesh=mesh,
            in_specs=(P(("grp", "comp"), None), P("comp", None), P("comp", None), P()),
            out_specs=(P(), P(), P(), P(("grp", "comp"))),
            check_vma=False,
        )(features, means, variances, weight_logits)

    return whole
```

```python
import functools
import math

import jax
import jax.numpy as jnp
import numpy as np
from jax import lax
from jax.experimental import pallas as pl
from jax.experimental.pallas import tpu as pltpu
from jax.sharding import PartitionSpec as P

F32 = jnp.float32
BF16 = jnp.bfloat16
LANES = 128
COUNT_ROWS = 8
LOG2E = math.log2(math.e)
LN2 = math.log(2.0)
BLOCK = 1024


class Plan:
    def __init__(self, groups, owners, comps):
        self.devices = groups * owners
        self.owners = owners
        owner_bits = owners.bit_length() - 1
        group_bits = groups.bit_length() - 1
        assert owners == 1 << owner_bits and groups == 1 << group_bits
        assert owner_bits >= 4 and group_bits >= 1 and comps % owners == 0
        self.units = owners
        self.unit = comps // owners
        self.masks = [1] + [1 << b | 1 for b in range(1, owner_bits)]
        self.masks += [1 << b for b in range(owner_bits, owner_bits + group_bits)]
        split = [1, owner_bits] + list(range(2, owner_bits - 1))
        rest = [b for b in range(1, owner_bits + group_bits) if b not in split]
        first, second, third, *others = split
        orders = (
            ((third, first, second), (second, third, first)),
            ((first, second, third), (second, third, first)),
        )
        self.halving = [
            [(0, 0)] + list(zip(zero, one)) + [(b, b) for b in others] for zero, one in orders
        ]
        self.whole = [(b, b) for b in rest]
        down = list(range(owner_bits - 1, 0, -1))
        self.gather = list(zip(down, down[:-2] + [down[-1], down[-2]]))

        def reach(device, steps, place):
            for t in reversed(range(len(steps))):
                if place >> t & 1:
                    device = self.partner(device, steps[t])
            return device

        def chunk(device):
            place = sum((device >> b & 1) << i for i, b in enumerate(split)) << 1
            return place | (self.colour(place) ^ self.colour(device))

        n = range(self.devices)
        places = range(self.units)
        unit_chunk = np.array([[reach(d, self.gather + [(0, 0)], p) % owners for p in places] for d in n])
        slot_chunk = [
            np.array([[chunk(reach(d, halving[::-1], j)) for j in places] for d in n]) for halving in self.halving
        ]
        unit_slot = [np.take_along_axis(np.argsort(c, axis=1), unit_chunk, axis=1) for c in slot_chunk]
        self.tables = np.stack([unit_chunk, *unit_slot, *slot_chunk], axis=1).astype(np.int32)

    def colour(self, device):
        return (device % self.owners).bit_count() & 1

    def partner(self, device, step):
        return device ^ self.masks[step[self.colour(device)]]

    def swap(self, value, step):
        pairs = [(d, self.partner(d, step)) for d in range(self.devices)]
        return lax.ppermute(value, ("grp", "comp"), pairs)


def columns(row, height):
    return jnp.broadcast_to(row, (height, LANES)).T


def start_kernel(plan, table, *refs):
    sources, (*copies, staged, logits_ref, sems) = refs[:3], refs[3:]
    targets = (*copies, logits_ref)
    moves = [pltpu.make_async_copy(s, t, sems.at[i]) for i, (s, t) in enumerate(zip(sources, targets))]
    for move in moves:
        move.start()
    for move in moves:
        move.wait()
    logits = logits_ref[...]
    shifted = logits - jnp.max(logits)
    log_weights = shifted - jnp.log(jnp.sum(jnp.exp(shifted)))
    for b in range(logits.shape[0]):
        staged[b * LANES : (b + 1) * LANES, :] = columns(log_weights[b : b + 1, :], LANES)


def stack_kernel(plan, table, source, stack_ref, features_ref, sems):
    count, width = features_ref.shape
    block = count // sems.shape[0]
    moves = []
    for at in range(sems.shape[0]):
        here = pl.ds(at * block, block)
        moves.append(pltpu.make_async_copy(source.at[here], features_ref.at[here], sems.at[at]))
        moves[-1].start()
    for at, move in enumerate(moves):
        move.wait()
        here = slice(at * block, (at + 1) * block)
        rows = features_ref[here, :]
        values = rows.astype(F32)
        squares = values * values
        high = squares.astype(BF16)
        stack_ref[here, :width] = (squares - high.astype(F32)).astype(BF16)
        stack_ref[here, width : 2 * width] = high
        stack_ref[here, 2 * width :] = rows


def build_weights(unit, table, first_units, mean_refs, variance_refs, log_weights, weights, offsets):
    at = 0
    width = mean_refs[0].shape[1]
    for mean_ref, variance_ref, first_unit in zip(mean_refs, variance_refs, first_units):
        for first in range(0, mean_ref.shape[0], unit):
            here = slice(at, at + unit)
            mean = mean_ref[first : first + unit, :]
            variance = variance_ref[first : first + unit, :]
            inverse = 1.0 / variance
            linear = mean * inverse
            constant = jnp.sum(jnp.log(variance) + mean * linear, axis=1, keepdims=True)
            chunk = pl.multiple_of(table[0, first_unit + first // unit] * unit, unit)
            log_weight = log_weights[pl.ds(chunk, unit), :]
            offsets[here, :] = (
                log_weight - 0.5 * constant - 0.5 * width * math.log(2.0 * math.pi)
            ) * LOG2E
            square = inverse * (-0.5 * LOG2E)
            linear = linear * LOG2E
            square_high = square.astype(BF16)
            linear_high = linear.astype(BF16)
            weights[here, :width] = square_high
            weights[here, width : 2 * width] = square_high
            weights[here, 2 * width : 3 * width] = linear_high
            weights[here, 3 * width : 4 * width] = (square - square_high.astype(F32)).astype(BF16)
            weights[here, 4 * width :] = (linear - linear_high.astype(F32)).astype(BF16)
            at += unit


def block_scores(stack, weights, offsets):
    width = stack.shape[1] // 3
    scores = lax.dot_general(
        weights[...],
        jnp.concatenate([stack, stack[:, width:]], axis=1),
        (((1,), (1,)), ((), ())),
        preferred_element_type=F32,
    )
    return scores + jnp.tile(offsets[...], (1, stack.shape[0] // LANES))


def store_moments(plan, table, first_unit, moments, targets):
    unit = plan.unit
    width = moments.shape[1] // 2
    parts = width // LANES
    for u in range(moments.shape[0] // unit):
        for column, target in enumerate(targets):
            slot = table[2 - column, first_unit + u] % (plan.units // 2)
            first = pl.multiple_of(slot * (unit * parts), unit)
            for part in range(parts):
                at = column * width + part * LANES
                target[pl.ds(first + part * unit, unit), :] = moments[
                    u * unit : (u + 1) * unit, at : at + LANES
                ]


def early_kernel(plan, first_units, table, *refs):
    pieces = len(first_units)
    mean_refs, variance_refs = refs[:pieces], refs[pieces : 2 * pieces]
    log_weights, stack_ref, powers_ref, highest_ref, totals_ref, weights, offsets = refs[2 * pieces :]
    count = stack_ref.shape[0]
    block = min(BLOCK, count)
    build_weights(plan.unit, table, first_units, mean_refs, variance_refs, log_weights, weights, offsets)
    for first in range(0, count, block):
        here = slice(first, first + block)
        scores = block_scores(stack_ref[here, :], weights, offsets)
        highest = jnp.max(scores, axis=0, keepdims=True)
        powers = jnp.exp2(scores - highest)
        powers_ref[:, here] = powers
        highest_ref[:, here] = highest
        totals_ref[:, here] = jnp.sum(powers, axis=0, keepdims=True)


def late_kernel(plan, table, *refs):
    mean_ref, variance_ref, log_weights, stack_ref = refs[:4]
    (powers_1, highest_1, totals_1), (powers_2, highest_2, totals_2) = refs[4:7], refs[7:10]
    sent_refs, counts_ref, scores_ref, own_ref = refs[10:12], refs[12], refs[13], refs[14]
    weights, offsets, moments, partial, staged = refs[15:]
    count, width = stack_ref.shape[0], stack_ref.shape[1] // 3
    block = min(2 * BLOCK, count)
    quarter = weights.shape[0]
    firsts = (3 * plan.units // 4,)
    build_weights(plan.unit, table, firsts, (mean_ref,), (variance_ref,), log_weights, weights, offsets)
    for first in range(0, count, block):
        here = slice(first, first + block)
        stack = stack_ref[here, :]
        scores = block_scores(stack, weights, offsets)
        highest = jnp.maximum(
            jnp.maximum(highest_1[:, here], highest_2[:, here]), jnp.max(scores, axis=0, keepdims=True)
        )
        scale_1 = jnp.exp2(highest_1[:, here] - highest)
        scale_2 = jnp.exp2(highest_2[:, here] - highest)
        powers = jnp.exp2(scores - highest)
        totals = (
            totals_1[:, here] * scale_1
            + totals_2[:, here] * scale_2
            + jnp.sum(powers, axis=0, keepdims=True)
        )
        scores_ref[:, here] = (highest + jnp.log2(totals)) * (LN2 / width)
        inverse = 1.0 / totals
        scale_1 = scale_1 * inverse
        scale_2 = scale_2 * inverse
        parts = (
            (powers_1[:quarter, here] * scale_1).astype(BF16),
            (powers_2[:, here] * scale_2).astype(BF16),
            (powers_1[quarter:, here] * scale_1).astype(BF16),
            (powers * inverse).astype(BF16),
        )
        own_ref[:quarter, here] = parts[0]
        own_ref[quarter:, here] = parts[1]
        added = jnp.dot(
            jnp.concatenate(parts[2:], axis=0),
            stack[:, width:],
            preferred_element_type=F32,
        )
        if first == 0:
            moments[...] = added
        else:
            moments[...] += added
        for at, part in enumerate(parts):
            rounded = part.astype(F32)
            counted = rounded[:, :LANES]
            for b in range(1, block // LANES):
                counted = counted + rounded[:, b * LANES : (b + 1) * LANES]
            here = slice(at * quarter, (at + 1) * quarter)
            if first == 0:
                partial[here, :] = counted
            else:
                partial[here, :] += counted

    unit = plan.unit
    for u in range(plan.units):
        chunk = pl.multiple_of(table[0, u] * unit, unit)
        staged[pl.ds(chunk, unit), :] = partial[u * unit : (u + 1) * unit, :]
    half = sent_refs[1].shape[0]
    for b in range(4 * quarter // LANES):
        line = jnp.sum(staged[b * LANES : (b + 1) * LANES, :].T, axis=0, keepdims=True)
        counts_ref[b : b + 1, :] = line
        sent_refs[0][half + b : half + b + 1, :] = line
    store_moments(plan, table, plan.units // 2, moments, sent_refs[::-1])


def own_kernel(plan, stream, table, own_ref, stack_ref, moments_ref):
    width = stack_ref.shape[1] // 3
    unit = plan.unit
    parts = width // LANES
    inputs = stack_ref[:, (2 - stream) * width : (3 - stream) * width]
    moments = jnp.dot(own_ref[...], inputs, preferred_element_type=F32)
    for u in range(plan.units // 2):
        slot = table[1 + stream, u] % (plan.units // 2)
        first = pl.multiple_of(slot * (unit * parts), unit)
        for part in range(parts):
            moments_ref[pl.ds(first + part * unit, unit), :] = moments[
                u * unit : (u + 1) * unit, part * LANES : (part + 1) * LANES
            ]


def call(kernel, plan, table, operands, shapes, scratch, flops, vmem_mib, space=pltpu.VMEM):
    vmem = pl.BlockSpec(memory_space=pltpu.VMEM)
    moved = sum(math.prod(o.shape) * o.dtype.itemsize for o in operands)
    return pl.pallas_call(
        functools.partial(kernel, plan),
        in_specs=[pl.BlockSpec(memory_space=pltpu.SMEM)] + [pl.BlockSpec(memory_space=space)] * len(operands),
        out_specs=[vmem] * len(shapes),
        out_shape=[jax.ShapeDtypeStruct(*s) for s in shapes],
        scratch_shapes=[pltpu.VMEM(*s) if isinstance(s, tuple) else s for s in scratch],
        compiler_params=pltpu.CompilerParams(vmem_limit_bytes=vmem_mib * 2**20),
        cost_estimate=pl.CostEstimate(flops=flops, bytes_accessed=2 * moved, transcendentals=0),
    )(table, *operands)


def in_hbm(arrays):
    return [pltpu.with_memory_space_constraint(a, pltpu.HBM) for a in arrays]


def own_copies(plan, table, means, variances, logits):
    return call(
        start_kernel,
        plan,
        table,
        in_hbm([means, variances, logits]),
        [(means.shape, F32)] * 2 + [((math.prod(logits.shape), LANES), F32)],
        [(logits.shape, F32), pltpu.SemaphoreType.DMA((3,))],
        0,
        8,
        pltpu.HBM,
    )


def feature_stack(plan, table, features):
    count, width = features.shape
    return call(
        stack_kernel,
        plan,
        table,
        in_hbm([features]),
        [((count, 3 * width), BF16)],
        [((count, width), BF16), pltpu.SemaphoreType.DMA((4,))],
        8 * count * width,
        16,
        pltpu.HBM,
    )[0]


def early_scores(plan, table, first_units, means, variances, log_weights, stack):
    count, width = stack.shape[0], stack.shape[1] // 3
    comps = sum(m.shape[0] for m in means)
    return call(
        lambda plan, *refs: early_kernel(plan, first_units, *refs),
        plan,
        table,
        [*means, *variances, log_weights, stack],
        [((comps, count), F32), ((1, count), F32), ((1, count), F32)],
        [((comps, 5 * width), BF16), ((comps, LANES), F32)],
        10 * comps * count * width,
        24,
    )


def mixture(plan, table, mean, variance, log_weights, stack, early):
    count, width = stack.shape[0], stack.shape[1] // 3
    half = 2 * mean.shape[0]
    rows = half * (width // LANES)
    *sent, counts, row_scores, own = call(
        late_kernel,
        plan,
        table,
        [mean, variance, log_weights, stack, *early],
        [
            ((rows + COUNT_ROWS, LANES), F32),
            ((rows, LANES), F32),
            ((COUNT_ROWS, LANES), F32),
            ((1, count), F32),
            ((half, count), BF16),
        ],
        [
            ((half // 2, 5 * width), BF16),
            ((half // 2, LANES), F32),
            ((half, 2 * width), F32),
            ((2 * half, LANES), F32),
            ((2 * half, LANES), F32),
        ],
        9 * half * count * width,
        32,
    )
    kept = [
        call(
            lambda plan, *refs, stream=stream: own_kernel(plan, stream, *refs),
            plan,
            table,
            [own, stack],
            [((rows, LANES), F32)],
            [],
            2 * half * count * width,
            16,
        )[0]
        for stream in (0, 1)
    ]
    return sent, kept, counts, row_scores


def scale_kernel(plan, total_rows, table, counts_ref, log_weights_ref, scale_ref):
    denominator = counts_ref[...] + 1.0
    log_weights_ref[...] = jnp.log(denominator / total_rows)
    inverse = 1.0 / denominator
    for b in range(counts_ref.shape[0]):
        scale_ref[b * LANES : (b + 1) * LANES, :] = columns(inverse[b : b + 1, :], LANES)


def update_kernel(plan, first_slot, table, *refs):
    piece_refs, scale_ref = (refs[:2], refs[2:4]), refs[4]
    means_ref, variances_ref, mean_buffer, variance_buffer, sems = refs[-5:]
    width = mean_buffer.shape[1]
    unit = plan.unit
    parts = width // LANES
    moves = []
    for stream, buffer, target in ((0, mean_buffer, means_ref), (1, variance_buffer, variances_ref)):
        slot = first_slot
        for ref in piece_refs[stream]:
            for first in range(0, ref.shape[0], unit * parts):
                chunk = pl.ds(pl.multiple_of(table[3 + stream, slot] * unit, unit), unit)
                scale = scale_ref[chunk, :]
                for part in range(parts):
                    lanes = slice(part * LANES, (part + 1) * LANES)
                    moment = ref[first + part * unit : first + (part + 1) * unit, :]
                    if stream == 0:
                        buffer[chunk, lanes] = moment * scale
                    else:
                        mean = mean_buffer[chunk, lanes]
                        buffer[chunk, lanes] = (moment + 1.0) * scale - mean * mean + 0.01
                sem = sems.at[stream, slot - first_slot]
                move = pltpu.make_async_copy(buffer.at[chunk, :], target.at[chunk, :], sem)
                move.start()
                moves.append(move)
                slot += 1
    for move in moves:
        move.wait()


def update(plan, table, first_slot, first, second, scale, shape, earlier=()):
    vmem = pl.BlockSpec(memory_space=pltpu.VMEM)
    hbm = pl.BlockSpec(memory_space=pl.ANY)
    operands = [*first, *second, scale]
    return pl.pallas_call(
        functools.partial(update_kernel, plan, first_slot),
        in_specs=[pl.BlockSpec(memory_space=pltpu.SMEM)] + [vmem] * len(operands) + [hbm] * len(earlier),
        out_specs=[hbm] * 2,
        out_shape=[jax.ShapeDtypeStruct(shape, F32)] * 2,
        scratch_shapes=[
            pltpu.VMEM(shape, F32),
            pltpu.VMEM(shape, F32),
            pltpu.SemaphoreType.DMA((2, plan.units // 2)),
        ],
        input_output_aliases={1 + len(operands) + i: i for i in range(len(earlier))},
        compiler_params=pltpu.CompilerParams(vmem_limit_bytes=16 * 2**20),
        cost_estimate=pl.CostEstimate(
            flops=4 * math.prod(shape), bytes_accessed=8 * math.prod(shape), transcendentals=0
        ),
    )(table, *operands, *earlier)


def double(plan, held, step, arrived=None):
    arrived = [plan.swap(h, at) for h, at in zip(held, step)] if arrived is None else arrived
    return [jnp.concatenate(pair, axis=0) for pair in zip(held, arrived)]


def scatter(plan, sent, kept, counts):
    rows = kept[1].shape[0]
    for at, step in enumerate(zip(*plan.halving)):
        if at:
            rows //= 2
            sent = [jnp.concatenate([kept[0][rows:], counts], axis=0), kept[1][rows:]]
            kept = [k[:rows] for k in kept]
        arrived = [plan.swap(s, pair) for s, pair in zip(sent, step)]
        counts = counts + arrived[0][rows:]
        kept = [k + a[:rows] for k, a in zip(kept, arrived)]
    for pair in plan.whole:
        arrived = [plan.swap(jnp.concatenate([kept[0], counts], axis=0), pair), plan.swap(kept[1], pair)]
        counts = counts + arrived[0][rows:]
        first = kept[0] + arrived[0][:rows]
        second, _ = lax.optimization_barrier((arrived[1], first))
        kept = [first, kept[1] + second]
    return kept, 0.5 * (counts + plan.swap(counts, (0, 0)))


def on_device(plan, features, means, variances, weight_logits):
    comps = weight_logits.shape[0]
    width = means.shape[1]
    me = lax.axis_index(("grp", "comp"))
    table = lax.dynamic_index_in_dim(jnp.asarray(plan.tables), me, 0, keepdims=False)
    logits = weight_logits.reshape(comps // LANES, LANES)

    with jax.named_scope("gather_parameters"):
        arrived = [plan.swap(h, plan.gather[0]) for h in (means, variances)]
        *held, log_weights = own_copies(plan, table, means, variances, logits)
        stack = feature_stack(plan, table, features)
        arrived[1], stack = lax.optimization_barrier((arrived[1], stack))
        held = double(plan, held, None, arrived)
        for step in plan.gather[1:-1]:
            held = double(plan, held, (step, step))
        last = [plan.swap(h, plan.gather[-1]) for h in held]
        both = lax.optimization_barrier(held)
        pairs = [(h, plan.swap(b, (0, 0))) for h, b in zip(held, both)]
        firsts = (0, plan.units // 2)
        early = early_scores(plan, table, firsts, *pairs, log_weights, stack)
        last[0], early = lax.optimization_barrier((last[0], early))
        mates = [plan.swap(l, (0, 0)) for l in last]
        firsts = (plan.units // 4,)
        early += early_scores(plan, table, firsts, last[:1], last[1:], log_weights, stack)
    sent, kept, counts, row_scores = mixture(plan, table, *mates, log_weights, stack, early)
    with jax.named_scope("scatter_moments"):
        kept, counts = scatter(plan, sent, kept, counts)
    with jax.named_scope("gather_moments"):
        total_rows = float(features.shape[0] * plan.devices + comps)
        log_weights, scale = call(
            lambda plan, *refs: scale_kernel(plan, total_rows, *refs),
            plan,
            table,
            [counts],
            [(counts.shape, F32), ((comps, LANES), F32)],
            [],
            comps,
            8,
        )
        steps = list(zip(*plan.halving))[:0:-1]
        held = kept
        for step in steps[:-1]:
            held = double(plan, held, step)
        last = [plan.swap(h, at) for h, at in zip(held, steps[-1])]
        mates = [plan.swap(h, (0, 0)) for h in held]
        last[0], scale = lax.optimization_barrier((last[0], scale))
        own = [[h, l] for h, l in zip(held, last)]
        others = [[m, plan.swap(l, (0, 0))] for m, l in zip(mates, last)]
    fresh = update(plan, table, 0, *own, scale, (comps, width))
    fresh_means, fresh_variances = update(
        plan, table, plan.units // 2, *others, scale, (comps, width), fresh
    )
    return fresh_means, fresh_variances, log_weights.reshape(comps), row_scores.reshape(-1)


def solution(mesh):
    def whole(features, means, variances, weight_logits):
        plan = Plan(mesh.shape["grp"], mesh.shape["comp"], weight_logits.shape[0])
        return jax.shard_map(
            functools.partial(on_device, plan),
            mesh=mesh,
            in_specs=(P(("grp", "comp"), None), P("comp", None), P("comp", None), P()),
            out_specs=(P(), P(), P(), P(("grp", "comp"))),
            check_vma=False,
        )(features, means, variances, weight_logits)

    return whole
```
